256 devices in a mesh: node: 4 (over y_hi, core), dp: 64 (over x, y_lo, z).
Axes of the slice: x: 4, y: 4 (y_hi: 2, y_lo: 2; y = y_hi * 2 + y_lo), z: 8, core: 2. Of those that a mesh axis runs over, the one named last changes fastest.
Arguments:
- tokens: bfloat16 [2, 65536, 8192], P(None, ('node', 'dp')), may hold values from -24 to 24
- cotangent: bfloat16 [2, 65536, 512], P(None, ('node', 'dp')), may hold values from -0.0390625 to 0.0390625
- master: float32 [8192, 512], P(('node', 'dp')), may hold values from -0.0625 to 0.0625
- moment: float32 [8192, 512], P(('node', 'dp')), may hold values from -6 to 6
- second: float32 [8192, 512], P(('node', 'dp')), may hold values from 0.25 to 4
- gradient: float32 [8192, 512], P(('node', 'dp')), may hold values from -6 to 6
Outputs:
- new_master: float32 [8192, 512], P(('node', 'dp'))
- new_moment: float32 [8192, 512], P(('node', 'dp'))
- new_second: float32 [8192, 512], P(('node', 'dp'))
- values: bfloat16 [2, 65536, 512], P(None, ('node', 'dp'))
- weight_grad: float32 [8192, 512], P(('node', 'dp'))
The draws below stay inside these ranges and needn't reach their ends.
All inputs are finite; a program needn't handle non-finite values.
Results may differ from the reference program's by a relative error of at most 0.0049.
Values may be sent and summed in bfloat16 or wider, within the bound.
No kernel may reach another device: no remote copies, remote signals or barrier semaphores. Data moves between devices by JAX's collectives and lax.ppermute only.
A program may use at most 128 MiB of HBM per device.

```python
import math
import jax
import jax.numpy as jnp

D = 8192
VW = 512
MICRO = 2
TOKENS = 65536


def raised(result, key, source, target, blocks, factor):
    owner, partner = [(jnp.arange(result.shape[axis_at]) // (result.shape[axis_at] // blocks)).reshape([-1 if axis == axis_at else 1 for axis in range(result.ndim)]) for axis_at in (source, target)]
    chosen = jax.random.permutation(key, blocks)[partner]
    strong = (owner == chosen) | (owner == (partner + blocks // 2) % blocks)
    return jnp.where(strong, factor * result, result)


def steps_of(key, dims, shards, smallest, largest):
    gain = 1.0
    for dim, shards_of in shards:
        heights = jax.random.uniform(jax.random.fold_in(jax.random.fold_in(key, 6), dim), (shards_of,), jnp.float32, smallest / len(shards), largest / len(shards))
        gain = gain * jnp.repeat(jnp.exp(heights), dims[dim] // shards_of).reshape((-1,) + (1,) * (len(dims) - 1 - dim))
    return gain


def gaussian(own_key, dims, scale, limit, cuts=(), dtype=jnp.bfloat16):
    result = scale * jax.random.normal(own_key, dims, jnp.float32)
    if cuts:
        result = result * steps_of(own_key, dims, cuts, -0.22, 0.18)
    return jnp.clip(result, -limit, limit).astype(dtype)


def heavy_noise(stream_key, extent, scale, reach, split, heavy, held_as=jnp.bfloat16):
    values = scale * jax.random.normal(stream_key, extent, jnp.float32)
    if split:
        values = values * steps_of(stream_key, extent, split, -0.22, 0.18)
    return jnp.clip(raised(values, jax.random.fold_in(stream_key, 3), *heavy), -reach, reach).astype(held_as)


def setup_inputs(seed: int = 0) -> dict:
    key_of = jax.random.split(jax.random.key(seed), 7)
    tokens = heavy_noise(key_of[0], (MICRO, TOKENS, D), 1.0, 24.0, ((1, 256),), (1, 2, 256, 6.0))
    cotangent = gaussian(key_of[1], (MICRO, TOKENS, VW), ((MICRO * TOKENS) ** -0.5), 0.0390625, ((1, 256),))
    master = gaussian(key_of[2], (D, VW), D ** -0.5, 0.0625, ((0, 256),), jnp.float32)
    moment = gaussian(key_of[3], (D, VW), 1.0, 6.0, ((0, 256),), jnp.float32)
    second = jnp.clip(jnp.exp(math.log(4.0) - 2.7725887 * jax.random.uniform(key_of[4], (D, VW), jnp.float32) ** steps_of(key_of[4], (D, VW), ((0, 256),), -0.2, 0.2)), 0.25, 4.0)
    gradient = gaussian(key_of[5], (D, VW), 1.0, 6.0, ((0, 256),), jnp.float32)
    return dict(tokens=tokens, cotangent=cotangent, master=master, moment=moment, second=second, gradient=gradient)


def reference(tokens, cotangent, master, moment, second, gradient):
    new_moment = 0.9 * moment + 0.1 * gradient
    new_second = 0.95 * second + 0.05 * gradient * gradient
    first_fix = 1.0 - 0.9 ** 10
    second_fix = 1.0 - 0.95 ** 10
    update = new_moment / first_fix / (jnp.sqrt(new_second / second_fix) + 1e-08) + 0.1 * master
    new_master = master - 0.001 * update
    weight = new_master.astype(jnp.bfloat16)
    flat_tokens = tokens.reshape(-1, D)
    flat_cot = cotangent.reshape(-1, VW)
    values = jnp.dot(flat_tokens, weight, preferred_element_type=jnp.float32).astype(jnp.bfloat16)
    values = values.reshape(MICRO, TOKENS, VW)
    weight_grad = jnp.dot(flat_tokens.T, flat_cot, preferred_element_type=jnp.float32)
    return (new_master, new_moment, new_second, values, weight_grad)
```

```python
import functools
import jax
import jax.numpy as jnp
from jax import lax
from jax.experimental import pallas as pl
from jax.experimental.pallas import tpu as pltpu
from jax.sharding import PartitionSpec as P

F32, BF16 = jnp.float32, jnp.bfloat16
ALL = ("node", "dp")
INTERPRET = False


def place(x, y, z, c):
    return ((((y // 2) * 2 + c) * 4 + x) * 2 + y % 2) * 8 + z


def devices():
    for c in range(2):
        for x in range(4):
            for y in range(4):
                for z in range(8):
                    yield x, y, z, c


def near_of(v, n, c):
    step = 1 - 2 * ((v + c) % 2)
    return (v + step) % n


def near(value, axis):
    pairs = []
    for x, y, z, c in devices():
        at = [x, y, z]
        at[axis] = near_of(at[axis], (4, 4, 8)[axis], c)
        pairs.append((place(x, y, z, c), place(*at, c)))
    return lax.ppermute(value, ALL, pairs)


def shift(value, dx, dy, dz):
    pairs = [
        (place(x, y, z, c), place((x + dx) % 4, (y + dy) % 4, (z + dz) % 8, c))
        for x, y, z, c in devices()
    ]
    return lax.ppermute(value, ALL, pairs)


def swap(value):
    pairs = [(place(x, y, z, c), place(x, y, z, 1 - c)) for x, y, z, c in devices()]
    return lax.ppermute(value, ALL, pairs)


def relative(u, v, n, c):
    p = lax.rem(u + v, 2)
    step = 1 - 2 * lax.rem(v + c, 2)
    d = lax.rem(u - v - p * step + 2 * n, n) // 2
    return p, d


def grad_kernel(me, own, r0, r1, cot, cotr, sx, sy, sz, kx, ky, kz):
    t = pl.program_id(0)
    yh, x = t // 4, lax.rem(t, 4)
    mx, my, mz, c = me[0], me[1], me[2], me[3]
    rows = own.shape[0] * own.shape[1]
    dims = (((0,), (0,)), ((), ()))

    def work(other):
        acc = lax.dot_general(
            own[...].reshape(rows, 512),
            cot[...].reshape(rows, 512),
            dims,
            preferred_element_type=F32,
        )
        acc += lax.dot_general(
            other[...].reshape(rows, 512),
            cotr[...].reshape(rows, 512),
            dims,
            preferred_element_type=F32,
        )
        px, dx = relative(x, mx, 4, c)
        ys = [relative(2 * yh + yl, my, 4, c) for yl in range(2)]
        zs = [relative(z, mz, 8, c) for z in range(8)]

        def part_x(block, yl, z):
            return block[0:16, 0:384], ys[yl][0] * 32 + zs[z][0] * 16 + dx * 8 + ys[yl][1] * 4 + zs[z][1]

        def part_y(block, yl, z):
            return block[16:32, 0:384], zs[z][0] * 32 + px * 16 + dx * 8 + ys[yl][1] * 4 + zs[z][1]

        def part_z(block, yl, z):
            return block[:, 384:512], px * 32 + ys[yl][0] * 16 + dx * 8 + ys[yl][1] * 4 + zs[z][1]

        def put(ref, part, yl, z):
            block = acc[(yl * 8 + z) * 32 : (yl * 8 + z) * 32 + 32]
            value, at = part(block, yl, z)
            ref[at] = value.astype(ref.dtype)

        everywhere = [(yl, z) for yl in range(2) for z in range(8)]
        for p, ref in ((0, kx), (1, sx)):

            @pl.when(px == p)
            def _(ref=ref):
                for yl, z in everywhere:
                    put(ref, part_x, yl, z)

        for yl in range(2):
            for p, ref in ((0, ky), (1, sy)):

                @pl.when(ys[yl][0] == p)
                def _(ref=ref, yl=yl):
                    for z in range(8):
                        put(ref, part_y, yl, z)

        for parity in range(2):

            @pl.when(lax.rem(mz, 2) == parity)
            def _(parity=parity):
                for yl, z in everywhere:
                    put(kz if z % 2 == parity else sz, part_z, yl, z)

    @pl.when(yh == 0)
    def _():
        work(r0)

    @pl.when(yh == 1)
    def _():
        work(r1)


def values_kernel(me, own0, own1, r0, r1, xa, xb, ya, yb, za, zb, keep, send, w):
    t = pl.program_id(0)
    mx, my, mz, c = me[0], me[1], me[2], me[3]

    @pl.when(t == 0)
    def _():
        def absolute(v, n, p, d):
            step = 1 - 2 * lax.rem(v + c, 2)
            return lax.rem(v + p * step + 2 * d + n, n)

        xs = [[absolute(mx, 4, p, d) * 512 for d in range(2)] for p in range(2)]
        ys = [[absolute(my, 4, p, d) for d in range(2)] for p in range(2)]
        ys = [[(y // 2) * 2048 + lax.rem(y, 2) * 256 for y in row] for row in ys]
        zs = [[absolute(mz, 8, p, d) * 32 for d in range(4)] for p in range(2)]
        far = [(dx, dy, dz) for dx in range(2) for dy in range(2) for dz in range(4)]
        for px in range(2):
            for py in range(2):
                for pz in range(2):
                    for i, (dx, dy, dz) in enumerate(far):
                        at = pl.multiple_of(xs[px][dx] + ys[py][dy] + zs[pz][dz], 32)
                        w[pl.ds(at, 16), 0:384] = (xa, xb)[px][py * 32 + pz * 16 + i]
                        w[pl.ds(at + 16, 16), 0:384] = (ya, yb)[py][pz * 32 + px * 16 + i]
                        w[pl.ds(at, 32), 384:512] = (za, zb)[pz][px * 32 + py * 16 + i]

    def product(a, b, out):
        out[0] = jnp.dot(a[0], w[0:2048], preferred_element_type=F32) + jnp.dot(
            b[0], w[2048:4096], preferred_element_type=F32
        )

    @pl.when(t < 2)
    def _():
        product(r0, r1, send)

    @pl.when(t >= 2)
    def _():
        product(own0, own1, keep)


def gradient_terms(me, tokens, r0, r1, cot, cotr):
    micro, rows, _ = tokens.shape
    block = (micro, rows, 512)
    vmem = pl.BlockSpec(memory_space=pltpu.VMEM)
    whole = pl.BlockSpec(block, lambda t, s: (0, 0, 0))
    shapes = [(64, 16, 384), (64, 16, 384), (64, 32, 128)]
    return pl.pallas_call(
        grad_kernel,
        grid_spec=pltpu.PrefetchScalarGridSpec(
            num_scalar_prefetch=1,
            grid=(8,),
            in_specs=[
                pl.BlockSpec(block, lambda t, s: (0, 0, (t // 4) * 8 + s[3] * 4 + t % 4)),
                pl.BlockSpec(block, lambda t, s: (0, 0, jnp.minimum(t, 3))),
                pl.BlockSpec(block, lambda t, s: (0, 0, jnp.maximum(t - 4, 0))),
                whole,
                whole,
            ],
            out_specs=[vmem] * 6,
        ),
        out_shape=[jax.ShapeDtypeStruct(s, BF16) for s in shapes]
        + [jax.ShapeDtypeStruct(s, F32) for s in shapes],
        compiler_params=pltpu.CompilerParams(vmem_limit_bytes=40 << 20),
        interpret=INTERPRET,
    )(me, tokens, r0, r1, cot, cotr)


def partial_values(me, tokens, r0, r1, halves):
    micro, rows, _ = tokens.shape
    vmem = pl.BlockSpec(memory_space=pltpu.VMEM)
    block = (1, rows, 2048)
    out = (1, rows, 512)
    shape = jax.ShapeDtypeStruct((micro, rows, 512), F32)
    return pl.pallas_call(
        values_kernel,
        grid_spec=pltpu.PrefetchScalarGridSpec(
            num_scalar_prefetch=1,
            grid=(4,),
            in_specs=[
                pl.BlockSpec(block, lambda t, s: (jnp.maximum(t - 2, 0), 0, s[3])),
                pl.BlockSpec(block, lambda t, s: (jnp.maximum(t - 2, 0), 0, 2 + s[3])),
                pl.BlockSpec(block, lambda t, s: (jnp.minimum(t, 1), 0, 0)),
                pl.BlockSpec(block, lambda t, s: (jnp.minimum(t, 1), 0, 0)),
            ]
            + [vmem] * 6,
            out_specs=[
                pl.BlockSpec(out, lambda t, s: (jnp.maximum(t - 2, 0), 0, 0)),
                pl.BlockSpec(out, lambda t, s: (jnp.minimum(t, 1), 0, 0)),
            ],
            scratch_shapes=[pltpu.VMEM((4096, 512), BF16)],
        ),
        out_shape=[shape, shape],
        compiler_params=pltpu.CompilerParams(vmem_limit_bytes=40 << 20),
        interpret=INTERPRET,
    )(me, tokens, tokens, r0, r1, *halves)


def gathered(weight):
    line = [weight] + [shift(weight, 0, 0, -2 * d) for d in (1, 2, 3)]
    line = jnp.stack(line)
    plane = [line] + [shift(line, 2 * (q // 2), 2 * (q % 2), 0) for q in (1, 2, 3)]

    def stream(cut, axes):
        held = jnp.concatenate([cut(part) for part in plane])
        for axis in axes[:2]:
            held = jnp.concatenate([held, near(held, axis)])
        return [held, near(held, axes[2])]

    return (
        stream(lambda a: a[:, 0:16, 0:384], (2, 1, 0))
        + stream(lambda a: a[:, 16:32, 0:384], (0, 2, 1))
        + stream(lambda a: a[:, :, 384:512], (1, 0, 2))
    )


def scattered(terms):
    def stream(send, keep, axes):
        for axis in axes:
            total = keep + near(send, axis).astype(F32)
            half = total.shape[0] // 2
            keep, send = total[:half], total[half:].astype(BF16)
        return total

    sx, sy, sz, kx, ky, kz = terms
    x = stream(sx, kx, (0, 1, 2))
    y = stream(sy, ky, (1, 2, 0))
    z = stream(sz, kz, (2, 0, 1))

    def joined(q):
        at = slice(4 * q, 4 * q + 4)
        return jnp.concatenate([jnp.concatenate([x[at], y[at]], axis=1), z[at]], axis=2)

    line = joined(0)
    for q in (1, 2, 3):
        line += shift(joined(q).astype(BF16), 2 * (q // 2), 2 * (q % 2), 0).astype(F32)
    total = line[0]
    for d in (1, 2, 3):
        total += shift(line[d].astype(BF16), 0, 0, 2 * d).astype(F32)
    return total


def body(tokens, cotangent, master, moment, second, gradient):
    node, dp = lax.axis_index("node"), lax.axis_index("dp")
    core = node % 2
    me = jnp.stack([dp // 16, (node // 2) * 2 + (dp // 8) % 2, dp % 8, core]).astype(jnp.int32)

    new_moment = 0.9 * moment + 0.1 * gradient
    new_second = 0.95 * second + 0.05 * gradient * gradient
    first_fix = 1.0 - 0.9**10
    second_fix = 1.0 - 0.95**10
    update = new_moment / first_fix / (jnp.sqrt(new_second / second_fix) + 1e-08) + 0.1 * master
    new_master = master - 0.001 * update
    weight = new_master.astype(BF16)

    far = 2048 * (1 - core)
    r0 = swap(lax.dynamic_slice_in_dim(tokens, far, 2048, 2))
    r1 = swap(lax.dynamic_slice_in_dim(tokens, far + 4096, 2048, 2))
    cotr = swap(cotangent)

    halves = gathered(weight)
    terms = gradient_terms(me, tokens, r0, r1, cotangent, cotr)
    weight_grad = scattered(terms)
    keep, send = partial_values(me, tokens, r0, r1, halves)
    values = (keep + swap(send)).astype(BF16)
    return (new_master, new_moment, new_second, values, weight_grad)


def solution(mesh):
    rows = P(("node", "dp"), None)
    tall = P(None, ("node", "dp"), None)
    return jax.shard_map(
        body,
        mesh=mesh,
        in_specs=(tall, tall, rows, rows, rows, rows),
        out_specs=(rows, rows, rows, tall, rows),
        check_vma=False,
    )
```

```python
import jax
import jax.numpy as jnp
from jax import lax
from jax.experimental import pallas as pl
from jax.experimental.pallas import tpu as pltpu
from jax.sharding import PartitionSpec as P

F32, BF16 = jnp.float32, jnp.bfloat16
ALL = ("node", "dp")
INTERPRET = False
VMEM = pl.BlockSpec(memory_space=pltpu.VMEM)
PARAMS = pltpu.CompilerParams(vmem_limit_bytes=40 << 20)


STREAMS = ((16, 384), (16, 384), (32, 128))
AXES = ((0, 1, 2), (1, 2, 0), (2, 0, 1))


def place(x, y, z, c):
    return ((((y // 2) * 2 + c) * 4 + x) * 2 + y % 2) * 8 + z


def permute(value, move):
    pairs = []
    for c in range(2):
        for x in range(4):
            for y in range(4):
                for z in range(8):
                    pairs.append((place(x, y, z, c), place(*move(x, y, z, c))))
    return lax.ppermute(value, ALL, pairs)


def neighbour(v, n, c):
    return (v + 1 - 2 * ((v + c) % 2)) % n


def near(value, axis):
    def move(x, y, z, c):
        at = [x, y, z]
        at[axis] = neighbour(at[axis], (4, 4, 8)[axis], c)
        return (*at, c)

    return permute(value, move)


def plane_step(value, xb, yb):
    def move(x, y, z, c):
        return (neighbour(x, 4, 1 - c) if xb else x, neighbour(y, 4, 1 - c) if yb else y, z, c)

    return permute(value, move)


def line_step(value, d):
    return permute(value, lambda x, y, z, c: (x, y, (z + d) % 8, c))


def swap(value):
    return permute(value, lambda x, y, z, c: (x, y, z, 1 - c))


def as_int(flag):
    return jnp.where(flag, 1, 0)


def label4(u, v, c):
    step = 1 - 2 * lax.rem(v + c, 2)
    delta = lax.rem(u - v + 4, 4)
    far = delta == 2
    return as_int(far | (delta == lax.rem(step + 4, 4))), as_int(far | (delta == lax.rem(4 - step, 4)))


def label8(u, v, c):
    p = lax.rem(u + v, 2)
    step = 1 - 2 * lax.rem(v + c, 2)
    return p, lax.rem(u - v - p * step + 16, 8) // 2


def reached4(v, c, a, b):
    step = 1 - 2 * lax.rem(v + c, 2)
    return lax.rem(v + (2 if a and b else a * step - b * step) + 4, 4)


def reached8(v, c, a, d):
    step = 1 - 2 * lax.rem(v + c, 2)
    return lax.rem(v + a * step + 2 * d + 8, 8)


def call(kernel, outs, *args, **more):
    return pl.pallas_call(
        kernel,
        out_shape=[jax.ShapeDtypeStruct(*o) for o in outs],
        in_specs=[VMEM] * len(args),
        out_specs=[VMEM] * len(outs),
        compiler_params=PARAMS,
        interpret=INTERPRET,
        **more,
    )(*args)


def first_kernel(me, tokens, master, moment, second, gradient, r0, r1, weight, out_master, out_moment, out_second, sems):
    far = pl.multiple_of(2048 * (1 - me[3]), 2048)
    copies = [
        pltpu.make_async_copy(tokens.at[:, :, pl.ds(far + 4096 * i, 2048)], ref, sems.at[i])
        for i, ref in enumerate((r0, r1))
    ]
    for copy in copies:
        copy.start()
    new_moment = 0.9 * moment[...] + 0.1 * gradient[...]
    new_second = 0.95 * second[...] + 0.05 * gradient[...] * gradient[...]
    first_fix = 1.0 - 0.9**10
    second_fix = 1.0 - 0.95**10
    update = new_moment / first_fix / (jnp.sqrt(new_second / second_fix) + 1e-08) + 0.1 * master[...]
    new_master = master[...] - 0.001 * update
    out_master[...] = new_master
    out_moment[...] = new_moment
    out_second[...] = new_second
    weight[...] = new_master.astype(BF16)
    for copy in copies:
        copy.wait()


def first(me, tokens, master, moment, second, gradient):
    half = jax.ShapeDtypeStruct((*tokens.shape[:2], 2048), BF16)
    rows = jax.ShapeDtypeStruct(master.shape, F32)
    return pl.pallas_call(
        first_kernel,
        in_specs=[pl.BlockSpec(memory_space=pltpu.SMEM), pl.BlockSpec(memory_space=pl.ANY)] + [VMEM] * 4,
        out_specs=[VMEM] * 6,
        out_shape=[half, half, jax.ShapeDtypeStruct(master.shape, BF16), rows, rows, rows],
        scratch_shapes=[pltpu.SemaphoreType.DMA((2,))],
        compiler_params=PARAMS,
        interpret=INTERPRET,
    )(me, tokens, master, moment, second, gradient)


def dot_rows(a, b):
    rows = a.shape[0] * a.shape[1]
    return lax.dot_general(
        a[...].reshape(rows, 512), b[...].reshape(rows, 512), (((0,), (0,)), ((), ())), preferred_element_type=F32
    )


def own_kernel(me, own, cot, out):
    out[pl.program_id(0)] = dot_rows(own, cot)


def own_terms(me, tokens, cot):
    block = (*tokens.shape[:2], 512)
    return pl.pallas_call(
        own_kernel,
        grid_spec=pltpu.PrefetchScalarGridSpec(
            num_scalar_prefetch=1,
            grid=(8,),
            in_specs=[
                pl.BlockSpec(block, lambda t, s: (0, 0, (t // 4) * 8 + s[3] * 4 + t % 4)),
                pl.BlockSpec(block, lambda t, s: (0, 0, 0)),
            ],
            out_specs=VMEM,
        ),
        out_shape=jax.ShapeDtypeStruct((8, 512, 512), F32),
        compiler_params=PARAMS,
        interpret=INTERPRET,
    )(me, tokens, cot)


def terms_kernel(me, r0, r1, cot, mine, sx, sy, sz, kx, ky, kz):
    t = pl.program_id(0)
    yh, x = t // 4, lax.rem(t, 4)
    mx, my, mz, c = me[0], me[1], me[2], me[3]

    def work(other):
        acc = mine[t] + dot_rows(other, cot)
        xa, xb = label4(x, mx, c)
        ys = [label4(2 * yh + yl, my, c) for yl in range(2)]
        zs = [label8(z, mz, c) for z in range(8)]

        def put(ref, stream, yl, z):
            near_at = (xa, ys[yl][0], zs[z][0])
            _, second, third = AXES[stream]
            at = near_at[second] * 32 + near_at[third] * 16 + xb * 8 + ys[yl][1] * 4 + zs[z][1]
            row = (yl * 8 + z) * 32
            part = (
                acc[row : row + 16, 0:384],
                acc[row + 16 : row + 32, 0:384],
                acc[row : row + 32, 384:512],
            )[stream]
            ref[at] = part.astype(ref.dtype)

        everywhere = [(yl, z) for yl in range(2) for z in range(8)]
        for sent, ref in ((0, kx), (1, sx)):

            @pl.when(xa == sent)
            def _(ref=ref):
                for yl, z in everywhere:
                    put(ref, 0, yl, z)

        for yl in range(2):
            for sent, ref in ((0, ky), (1, sy)):

                @pl.when(ys[yl][0] == sent)
                def _(ref=ref, yl=yl):
                    for z in range(8):
                        put(ref, 1, yl, z)

        for parity in range(2):

            @pl.when(lax.rem(mz, 2) == parity)
            def _(parity=parity):
                for yl, z in everywhere:
                    put(kz if z % 2 == parity else sz, 2, yl, z)

    @pl.when(yh == 0)
    def _():
        work(r0)

    @pl.when(yh == 1)
    def _():
        work(r1)


def all_terms(me, r0, r1, cot, mine):
    block = (*r0.shape[:2], 512)
    return pl.pallas_call(
        terms_kernel,
        grid_spec=pltpu.PrefetchScalarGridSpec(
            num_scalar_prefetch=1,
            grid=(8,),
            in_specs=[
                pl.BlockSpec(block, lambda t, s: (0, 0, jnp.minimum(t, 3))),
                pl.BlockSpec(block, lambda t, s: (0, 0, jnp.maximum(t - 4, 0))),
                pl.BlockSpec(block, lambda t, s: (0, 0, 0)),
                VMEM,
            ],
            out_specs=[VMEM] * 6,
        ),
        out_shape=[jax.ShapeDtypeStruct((80, *s), BF16) for s in STREAMS]
        + [jax.ShapeDtypeStruct((64, *s), F32) for s in STREAMS],
        compiler_params=PARAMS,
        interpret=INTERPRET,
    )(me, r0, r1, cot, mine)


def cut(stream, block):
    return (block[..., 0:16, 0:384], block[..., 16:32, 0:384], block[..., :, 384:512])[stream]


def pack_kernel(*refs):
    plane, outs = refs[3:7], refs[7:10]
    for stream, out in enumerate(outs):
        for q, part in enumerate(plane):
            out[64 + 4 * q : 68 + 4 * q] = cut(stream, part[...])


def second_kernel(sent, got, keep, send, kept):
    send[0:32] = (keep[32:64] + got[32:64].astype(F32)).astype(BF16)
    send[32:48] = sent[64:80]
    send[48:64] = got[64:80]
    kept[...] = keep[0:32] + got[0:32].astype(F32)


def third_kernel(sent, got, keep, send, kept):
    send[0:16] = (keep[16:32] + got[16:32].astype(F32)).astype(BF16)
    send[16:48] = sent[32:64]
    send[48:80] = got[32:64]
    kept[...] = keep[0:16] + got[0:16].astype(F32)


def far_kernel(gx, gy, gz, kx, ky, kz, own, s1, s2, s3):
    for q, out in enumerate((own, s1, s2, s3)):
        at = slice(4 * q, 4 * q + 4)
        out[:, 0:16, 0:384] = (kx[at] + gx[at].astype(F32)).astype(out.dtype)
        out[:, 16:32, 0:384] = (ky[at] + gy[at].astype(F32)).astype(out.dtype)
        out[:, :, 384:512] = (kz[at] + gz[at].astype(F32)).astype(out.dtype)


def last_kernel(own, g1, g2, g3, kept, s1, s2, s3):
    for d, out in enumerate((kept, s1, s2, s3)):
        total = own[d] + g1[d].astype(F32) + g2[d].astype(F32) + g3[d].astype(F32)
        out[...] = total.astype(out.dtype)


def sum_kernel(own, g1, g2, g3, out):
    out[...] = own[...] + g1[...].astype(F32) + g2[...].astype(F32) + g3[...].astype(F32)


def assemble(me, sx, sy, sz, gx, gy, gz, w):
    mx, my, mz, c = me[0], me[1], me[2], me[3]
    xs = [[reached4(mx, c, a, b) * 512 for b in range(2)] for a in range(2)]
    ys = [[reached4(my, c, a, b) for b in range(2)] for a in range(2)]
    ys = [[(y // 2) * 2048 + lax.rem(y, 2) * 256 for y in row] for row in ys]
    zs = [[reached8(mz, c, a, d) * 32 for d in range(4)] for a in range(2)]
    for xa in range(2):
        for ya in range(2):
            for za in range(2):
                for i in range(16):
                    at = pl.multiple_of(xs[xa][i // 8] + ys[ya][(i // 4) % 2] + zs[za][i % 4], 32)
                    label = (xa, ya, za)

                    def part(stream, sent, got):
                        first, second, third = (label[axis] for axis in AXES[stream])
                        return (got if third else sent)[16 + second * 32 + first * 16 + i]

                    w[pl.ds(at, 16), 0:384] = part(0, sx, gx)
                    w[pl.ds(at + 16, 16), 0:384] = part(1, sy, gy)
                    w[pl.ds(at, 32), 384:512] = part(2, sz, gz)


def product(a, b, w):
    return jnp.dot(a[0], w[0:2048], preferred_element_type=F32) + jnp.dot(
        b[0], w[2048:4096], preferred_element_type=F32
    )


def other_kernel(me, r0, r1, sx, sy, sz, gx, gy, gz, out, w):
    @pl.when(pl.program_id(0) == 0)
    def _():
        assemble(me, sx, sy, sz, gx, gy, gz, w)

    out[0] = product(r0, r1, w)


def mine_kernel(me, own0, own1, w, out):
    out[0] = product(own0, own1, w)


def other_values(me, r0, r1, messages):
    micro, rows, _ = r0.shape
    block = (1, rows, 2048)
    return pl.pallas_call(
        other_kernel,
        grid_spec=pltpu.PrefetchScalarGridSpec(
            num_scalar_prefetch=1,
            grid=(micro,),
            in_specs=[pl.BlockSpec(block, lambda t, s: (t, 0, 0))] * 2 + [VMEM] * 6,
            out_specs=[pl.BlockSpec((1, rows, 512), lambda t, s: (t, 0, 0)), VMEM],
        ),
        out_shape=[
            jax.ShapeDtypeStruct((micro, rows, 512), F32),
            jax.ShapeDtypeStruct((4096, 512), BF16),
        ],
        compiler_params=PARAMS,
        interpret=INTERPRET,
    )(me, r0, r1, *messages)


def my_values(me, tokens, w):
    micro, rows, _ = tokens.shape
    block = (1, rows, 2048)
    return pl.pallas_call(
        mine_kernel,
        grid_spec=pltpu.PrefetchScalarGridSpec(
            num_scalar_prefetch=1,
            grid=(micro,),
            in_specs=[
                pl.BlockSpec(block, lambda t, s: (t, 0, s[3])),
                pl.BlockSpec(block, lambda t, s: (t, 0, 2 + s[3])),
                VMEM,
            ],
            out_specs=pl.BlockSpec((1, rows, 512), lambda t, s: (t, 0, 0)),
        ),
        out_shape=jax.ShapeDtypeStruct((micro, rows, 512), F32),
        compiler_params=PARAMS,
        interpret=INTERPRET,
    )(me, tokens, tokens, w)


def after(value, *others):
    return lax.optimization_barrier((value, *others))[0]


def body(tokens, cotangent, master, moment, second, gradient):
    node, dp = lax.axis_index("node"), lax.axis_index("dp")
    me = jnp.stack([dp // 16, (node // 2) * 2 + (dp // 8) % 2, dp % 8, node % 2]).astype(jnp.int32)

    r0, r1, weight, new_master, new_moment, new_second = first(me, tokens, master, moment, second, gradient)
    r0, r1, cotr = swap(r0), swap(r1), swap(cotangent)
    line = jnp.stack([weight] + [line_step(weight, -2 * d) for d in (1, 2, 3)])
    mine = own_terms(me, tokens, cotangent)
    line = after(line, mine)
    plane = [line] + [plane_step(line, q // 2, q % 2) for q in (1, 2, 3)]
    terms = all_terms(me, r0, r1, cotr, mine)
    send, keep = terms[:3], terms[3:]

    send = call(
        pack_kernel,
        [((80, *s), BF16) for s in STREAMS],
        *send,
        *plane,
        input_output_aliases={0: 0, 1: 1, 2: 2},
    )
    got = [near(send[i], AXES[i][0]) for i in range(3)]
    for step, kernel, size, rest in ((1, second_kernel, 64, 32), (2, third_kernel, 80, 16)):
        new = [
            call(kernel, [((size, *STREAMS[i]), BF16), ((rest, *STREAMS[i]), F32)], send[i], got[i], keep[i])
            for i in range(3)
        ]
        send, keep = [n[0] for n in new], [n[1] for n in new]
        got = [near(send[i], AXES[i][step]) for i in range(3)]

    block = (4, 32, 512)
    own, *parts = call(far_kernel, [(block, F32)] + [(block, BF16)] * 3, *got, *keep)
    parts = [plane_step(part, q // 2, q % 2) for q, part in zip((1, 2, 3), parts)]

    other, w = other_values(me, r0, r1, [*send, *got])

    own, *parts = call(last_kernel, [(block[1:], F32)] + [(block[1:], BF16)] * 3, own, *parts)
    parts = [line_step(part, 2 * d) for d, part in zip((1, 2, 3), parts)]
    (weight_grad,) = call(sum_kernel, [(block[1:], F32)], own, *parts)

    ours = my_values(me, tokens, w)
    values = (ours + swap(other)).astype(BF16)
    return (new_master, new_moment, new_second, values, weight_grad)


def solution(mesh):
    rows = P(("node", "dp"), None)
    tall = P(None, ("node", "dp"), None)
    return jax.shard_map(
        body,
        mesh=mesh,
        in_specs=(tall, tall, rows, rows, rows, rows),
        out_specs=(rows, rows, rows, tall, rows),
        check_vma=False,
    )
```

```python
import jax
import jax.numpy as jnp
from jax import lax
from jax.experimental import pallas as pl
from jax.experimental.pallas import tpu as pltpu
from jax.sharding import PartitionSpec as P

F32, BF16 = jnp.float32, jnp.bfloat16
ALL = ("node", "dp")
INTERPRET = False
VMEM = pl.BlockSpec(memory_space=pltpu.VMEM)
SMEM = pl.BlockSpec(memory_space=pltpu.SMEM)
HBM = pl.BlockSpec(memory_space=pltpu.HBM)
PARAMS = pltpu.CompilerParams(vmem_limit_bytes=40 << 20)


STREAMS = ((16, 384), (16, 384), (32, 128))
AXES = ((0, 1, 2), (1, 2, 0), (2, 0, 1))


def place(x, y, z, c):
    return ((((y // 2) * 2 + c) * 4 + x) * 2 + y % 2) * 8 + z


def permute(value, move):
    pairs = []
    for c in range(2):
        for x in range(4):
            for y in range(4):
                for z in range(8):
                    pairs.append((place(x, y, z, c), place(*move(x, y, z, c))))
    return lax.ppermute(value, ALL, pairs)


def neighbour(v, n, c):
    return (v + 1 - 2 * ((v + c) % 2)) % n


def near(value, axis):
    def move(x, y, z, c):
        at = [x, y, z]
        at[axis] = neighbour(at[axis], (4, 4, 8)[axis], c)
        return (*at, c)

    return permute(value, move)


def plane_step(value, xb, yb):
    def move(x, y, z, c):
        return (neighbour(x, 4, 1 - c) if xb else x, neighbour(y, 4, 1 - c) if yb else y, z, c)

    return permute(value, move)


def line_step(value, d):
    return permute(value, lambda x, y, z, c: (x, y, (z + d) % 8, c))


def swap(value):
    return permute(value, lambda x, y, z, c: (x, y, z, 1 - c))


def as_int(flag):
    return jnp.where(flag, 1, 0)


def label4(u, v, c):
    step = 1 - 2 * lax.rem(v + c, 2)
    delta = lax.rem(u - v + 4, 4)
    far = delta == 2
    return as_int(far | (delta == lax.rem(step + 4, 4))), as_int(far | (delta == lax.rem(4 - step, 4)))


def label8(u, v, c):
    p = lax.rem(u + v, 2)
    step = 1 - 2 * lax.rem(v + c, 2)
    return p, lax.rem(u - v - p * step + 16, 8) // 2


def reached4(v, c, a, b):
    step = 1 - 2 * lax.rem(v + c, 2)
    return lax.rem(v + (2 if a and b else a * step - b * step) + 4, 4)


def reached8(v, c, a, d):
    step = 1 - 2 * lax.rem(v + c, 2)
    return lax.rem(v + a * step + 2 * d + 8, 8)


def call(kernel, outs, *args, **more):
    return pl.pallas_call(
        kernel,
        out_shape=[jax.ShapeDtypeStruct(*o) for o in outs],
        in_specs=[VMEM] * len(args),
        out_specs=[VMEM] * len(outs),
        compiler_params=PARAMS,
        interpret=INTERPRET,
        **more,
    )(*args)


def first_kernel(me, tokens, master, moment, second, gradient, r0, r1, weight, out_master, out_moment, out_second, rows, sems):
    far = pl.multiple_of(2048 * (1 - me[3]), 2048)
    loads = [
        pltpu.make_async_copy(ref, rows.at[i], sems.at[i]) for i, ref in enumerate((master, moment, second, gradient))
    ]
    copies = [
        pltpu.make_async_copy(tokens.at[:, :, pl.ds(far + 4096 * i, 2048)], ref, sems.at[4 + i])
        for i, ref in enumerate((r0, r1))
    ]
    for copy in loads + copies:
        copy.start()
    for copy in loads:
        copy.wait()
    new_moment = 0.9 * rows[1] + 0.1 * rows[3]
    new_second = 0.95 * rows[2] + 0.05 * rows[3] * rows[3]
    first_fix = 1.0 - 0.9**10
    second_fix = 1.0 - 0.95**10
    update = new_moment / first_fix / (jnp.sqrt(new_second / second_fix) + 1e-08) + 0.1 * rows[0]
    new_master = rows[0] - 0.001 * update
    out_master[...] = new_master
    out_moment[...] = new_moment
    out_second[...] = new_second
    weight[...] = new_master.astype(BF16)
    for copy in copies:
        copy.wait()


def first(me, tokens, master, moment, second, gradient):
    half = jax.ShapeDtypeStruct((*tokens.shape[:2], 2048), BF16)
    rows = jax.ShapeDtypeStruct(master.shape, F32)
    return pl.pallas_call(
        first_kernel,
        in_specs=[SMEM] + [HBM] * 5,
        out_specs=[VMEM] * 6,
        out_shape=[half, half, jax.ShapeDtypeStruct(master.shape, BF16), rows, rows, rows],
        scratch_shapes=[pltpu.VMEM((4, *master.shape), F32), pltpu.SemaphoreType.DMA((6,))],
        compiler_params=PARAMS,
        interpret=INTERPRET,
    )(me, tokens, master, moment, second, gradient)


def terms_kernel(me, tokens, r0, r1, cot, cotr, sx, sy, sz, kx, ky, kz, own, sems):
    mx, my, mz, c = me[0], me[1], me[2], me[3]
    mine = pl.multiple_of(2048 * c, 2048)
    loads = [
        pltpu.make_async_copy(tokens.at[:, :, pl.ds(mine + 4096 * (t // 4) + 512 * (t % 4), 512)], own.at[t], sems.at[t])
        for t in range(8)
    ]
    for load in loads:
        load.start()
    flat = cot.shape[0] * cot.shape[1]
    ours, theirs = cot[...].reshape(flat, 512), cotr[...].reshape(flat, 512)
    xs = [label4(x, mx, c) for x in range(4)]
    ys = [label4(y, my, c) for y in range(4)]
    zs = [label8(z, mz, c) for z in range(8)]

    def product(a, b):
        return lax.dot_general(a.reshape(flat, 512), b, (((0,), (0,)), ((), ())), preferred_element_type=F32)

    for t in range(8):
        other = (r0, r1)[t // 4][:, :, 512 * (t % 4) : 512 * (t % 4) + 512]
        acc = product(other, theirs)
        loads[t].wait()
        acc += product(own[t], ours)
        for j in range(16):
            x, y, z = xs[t % 4], ys[2 * (t // 4) + j // 8], zs[j % 8]
            far = x[1] * 8 + y[1] * 4 + z[1]
            axes = (x[0], y[0], z[0])
            block = acc[32 * j : 32 * j + 32]
            for stream, (send, keep) in enumerate(((sx, kx), (sy, ky), (sz, kz))):
                first_, second_, third_ = (axes[axis] for axis in AXES[stream])
                at = second_ * 32 + third_ * 16 + far
                part = cut(stream, block)
                send[jnp.where(first_ == 1, at, 64)] = part.astype(BF16)
                keep[jnp.where(first_ == 1, 64, at)] = part


def all_terms(me, tokens, r0, r1, cot, cotr):
    return pl.pallas_call(
        terms_kernel,
        in_specs=[SMEM, HBM] + [VMEM] * 4,
        out_specs=[VMEM] * 6,
        out_shape=[jax.ShapeDtypeStruct((80, *s), BF16) for s in STREAMS]
        + [jax.ShapeDtypeStruct((65, *s), F32) for s in STREAMS],
        scratch_shapes=[pltpu.VMEM((8, *tokens.shape[:2], 512), BF16), pltpu.SemaphoreType.DMA((8,))],
        compiler_params=PARAMS,
        interpret=INTERPRET,
    )(me, tokens, r0, r1, cot, cotr)


def cut(stream, block):
    return (block[..., 0:16, 0:384], block[..., 16:32, 0:384], block[..., :, 384:512])[stream]


def pack_kernel(*refs):
    plane, outs = refs[3:7], refs[7:10]
    for stream, out in enumerate(outs):
        for q, part in enumerate(plane):
            out[64 + 4 * q : 68 + 4 * q] = cut(stream, part[...])


def second_kernel(sent, got, keep, send, kept):
    send[0:32] = (keep[32:64] + got[32:64].astype(F32)).astype(BF16)
    send[32:48] = sent[64:80]
    send[48:64] = got[64:80]
    kept[...] = keep[0:32] + got[0:32].astype(F32)


def third_kernel(sent, got, keep, send, kept):
    send[0:16] = (keep[16:32] + got[16:32].astype(F32)).astype(BF16)
    send[16:48] = sent[32:64]
    send[48:80] = got[32:64]
    kept[...] = keep[0:16] + got[0:16].astype(F32)


def far_kernel(gx, gy, gz, kx, ky, kz, own, s1, s2, s3):
    for q, out in enumerate((own, s1, s2, s3)):
        at = slice(4 * q, 4 * q + 4)
        out[:, 0:16, 0:384] = (kx[at] + gx[at].astype(F32)).astype(out.dtype)
        out[:, 16:32, 0:384] = (ky[at] + gy[at].astype(F32)).astype(out.dtype)
        out[:, :, 384:512] = (kz[at] + gz[at].astype(F32)).astype(out.dtype)


def last_kernel(own, g1, g2, g3, kept, s1, s2, s3):
    for d, out in enumerate((kept, s1, s2, s3)):
        total = own[d] + g1[d].astype(F32) + g2[d].astype(F32) + g3[d].astype(F32)
        out[...] = total.astype(out.dtype)


def sum_kernel(own, g1, g2, g3, out):
    out[...] = own[...] + g1[...].astype(F32) + g2[...].astype(F32) + g3[...].astype(F32)


def assemble(me, sx, sy, sz, gx, gy, gz, w):
    mx, my, mz, c = me[0], me[1], me[2], me[3]
    xs = [[reached4(mx, c, a, b) * 512 for b in range(2)] for a in range(2)]
    ys = [[reached4(my, c, a, b) for b in range(2)] for a in range(2)]
    ys = [[(y // 2) * 2048 + lax.rem(y, 2) * 256 for y in row] for row in ys]
    zs = [[reached8(mz, c, a, d) * 32 for d in range(4)] for a in range(2)]
    for xa in range(2):
        for ya in range(2):
            for za in range(2):
                for i in range(16):
                    at = pl.multiple_of(xs[xa][i // 8] + ys[ya][(i // 4) % 2] + zs[za][i % 4], 32)
                    label = (xa, ya, za)

                    def part(stream, sent, got):
                        first, second, third = (label[axis] for axis in AXES[stream])
                        return (got if third else sent)[16 + second * 32 + first * 16 + i]

                    w[pl.ds(at, 16), 0:384] = part(0, sx, gx)
                    w[pl.ds(at + 16, 16), 0:384] = part(1, sy, gy)
                    w[pl.ds(at, 32), 384:512] = part(2, sz, gz)


def other_kernel(me, r0, r1, sx, sy, sz, gx, gy, gz, out, w):
    assemble(me, sx, sy, sz, gx, gy, gz, w)
    for m in range(out.shape[0]):
        out[m] = jnp.dot(r0[m], w[0:2048], preferred_element_type=F32) + jnp.dot(
            r1[m], w[2048:4096], preferred_element_type=F32
        )


def mine_kernel(me, tokens, w, other, out, own, sems):
    mine = pl.multiple_of(2048 * me[3], 2048)
    loads = [
        [
            pltpu.make_async_copy(tokens.at[m, :, pl.ds(mine + 4096 * i, 2048)], own.at[2 * m + i], sems.at[2 * m + i])
            for i in range(2)
        ]
        for m in range(2)
    ]
    for load in loads[0] + loads[1]:
        load.start()
    for m in range(2):
        total = other[m]
        for i in range(2):
            loads[m][i].wait()
            total += jnp.dot(own[2 * m + i], w[2048 * i : 2048 * i + 2048], preferred_element_type=F32)
        out[m] = total.astype(BF16)


def other_values(me, r0, r1, messages):
    return pl.pallas_call(
        other_kernel,
        in_specs=[SMEM] + [VMEM] * 8,
        out_specs=[VMEM] * 2,
        out_shape=[
            jax.ShapeDtypeStruct((*r0.shape[:2], 512), F32),
            jax.ShapeDtypeStruct((4096, 512), BF16),
        ],
        compiler_params=PARAMS,
        interpret=INTERPRET,
    )(me, r0, r1, *messages)


def my_values(me, tokens, w, other):
    micro, rows, _ = tokens.shape
    return pl.pallas_call(
        mine_kernel,
        in_specs=[SMEM, HBM, VMEM, VMEM],
        out_specs=VMEM,
        out_shape=jax.ShapeDtypeStruct((micro, rows, 512), BF16),
        scratch_shapes=[pltpu.VMEM((2 * micro, rows, 2048), BF16), pltpu.SemaphoreType.DMA((2 * micro,))],
        compiler_params=PARAMS,
        interpret=INTERPRET,
    )(me, tokens, w, other)


def after(value, *others):
    return lax.optimization_barrier((value, *others))[0]


def body(tokens, cotangent, master, moment, second, gradient):
    node, dp = lax.axis_index("node"), lax.axis_index("dp")
    me = jnp.stack([dp // 16, (node // 2) * 2 + (dp // 8) % 2, dp % 8, node % 2]).astype(jnp.int32)

    tokens, master, moment, second, gradient = (
        pltpu.with_memory_space_constraint(a, pltpu.HBM) for a in (tokens, master, moment, second, gradient)
    )
    r0, r1, weight, new_master, new_moment, new_second = first(me, tokens, master, moment, second, gradient)
    r0, r1, cotr = swap(r0), swap(r1), swap(cotangent)
    line = jnp.stack([weight] + [line_step(weight, -2 * d) for d in (1, 2, 3)])
    plane = [line] + [plane_step(line, q // 2, q % 2) for q in (1, 2, 3)]
    terms = all_terms(me, tokens, r0, r1, cotangent, cotr)
    send, keep = terms[:3], terms[3:]

    send = call(
        pack_kernel,
        [((80, *s), BF16) for s in STREAMS],
        *send,
        *plane,
        input_output_aliases={0: 0, 1: 1, 2: 2},
    )
    got = [near(send[i], AXES[i][0]) for i in range(3)]
    for step, kernel, size, rest in ((1, second_kernel, 64, 32), (2, third_kernel, 80, 16)):
        new = [
            call(kernel, [((size, *STREAMS[i]), BF16), ((rest, *STREAMS[i]), F32)], send[i], got[i], keep[i])
            for i in range(3)
        ]
        send, keep = [n[0] for n in new], [n[1] for n in new]
        got = [near(send[i], AXES[i][step]) for i in range(3)]

    block = (4, 32, 512)
    own, *parts = call(far_kernel, [(block, F32)] + [(block, BF16)] * 3, *got, *keep)
    parts = [plane_step(part, q // 2, q % 2) for q, part in zip((1, 2, 3), parts)]

    other, w = other_values(after(me, own), r0, r1, [*send, *got])
    other = swap(after(other, *parts))

    own, *parts = call(last_kernel, [(block[1:], F32)] + [(block[1:], BF16)] * 3, after(own, w), *parts)
    parts = [line_step(part, 2 * d) for d, part in zip((1, 2, 3), parts)]
    values = my_values(me, tokens, w, other)
    (weight_grad,) = call(sum_kernel, [(block[1:], F32)], after(own, values), *parts)
    return (new_master, new_moment, new_second, values, weight_grad)


def solution(mesh):
    rows = P(("node", "dp"), None)
    tall = P(None, ("node", "dp"), None)
    return jax.shard_map(
        body,
        mesh=mesh,
        in_specs=(tall, tall, rows, rows, rows, rows),
        out_specs=(rows, rows, rows, tall, rows),
        check_vma=False,
    )
```

```python
import functools
import jax
import jax.numpy as jnp
from jax import lax
from jax.experimental import pallas as pl
from jax.experimental.pallas import tpu as pltpu
from jax.sharding import PartitionSpec as P

F32, BF16 = jnp.float32, jnp.bfloat16
ALL = ("node", "dp")
INTERPRET = False
VMEM = pl.BlockSpec(memory_space=pltpu.VMEM)
SMEM = pl.BlockSpec(memory_space=pltpu.SMEM)
HBM = pl.BlockSpec(memory_space=pltpu.HBM)
PARAMS = pltpu.CompilerParams(vmem_limit_bytes=28 << 20)


STREAMS = ((16, 384), (16, 384), (32, 128))
AXES = ((0, 1, 2), (1, 2, 0), (2, 0, 1))


def message(n, stream):
    return (n + n // 2 if stream == 2 else n, *STREAMS[stream]), BF16


def place(x, y, z, c):
    return ((((y // 2) * 2 + c) * 4 + x) * 2 + y % 2) * 8 + z


def permute(value, move):
    pairs = []
    for c in range(2):
        for x in range(4):
            for y in range(4):
                for z in range(8):
                    pairs.append((place(x, y, z, c), place(*move(x, y, z, c))))
    return lax.ppermute(value, ALL, pairs)


def neighbour(v, n, c):
    return (v + 1 - 2 * ((v + c) % 2)) % n


def near(value, axis):
    def move(x, y, z, c):
        at = [x, y, z]
        at[axis] = neighbour(at[axis], (4, 4, 8)[axis], c)
        return (*at, c)

    return permute(value, move)


def far_step(value, axis, second):
    def move(x, y, z, c):
        at = [x, y, z]
        if axis < 2:
            at[axis] = neighbour(at[axis], 4, 1 - c)
        else:
            w = neighbour((z + c) // 2 % 4, 4, (1 - c) if second else c)
            at[2] = (2 * w + (z % 2) * (1 - 2 * c)) % 8
        return (*at, c)

    return permute(value, move)


def swap(value):
    return permute(value, lambda x, y, z, c: (x, y, z, 1 - c))


def as_int(flag):
    return jnp.where(flag, 1, 0)


def label4(u, v, c):
    step = 1 - 2 * lax.rem(v + c, 2)
    delta = lax.rem(u - v + 4, 4)
    far = delta == 2
    return as_int(far | (delta == lax.rem(step + 4, 4))), as_int(far | (delta == lax.rem(4 - step, 4)))


def label8(u, v, c):
    b, d = label4(lax.rem((u + c) // 2, 4), lax.rem((v + c) // 2, 4), c)
    return lax.rem(u + v, 2), b * 2 + d


def reached4(v, c, a, b):
    step = 1 - 2 * lax.rem(v + c, 2)
    return lax.rem(v + (2 if a and b else a * step - b * step) + 4, 4)


def reached8(v, c, a, d):
    w = reached4(lax.rem((v + c) // 2, 4), c, d // 2, d % 2)
    p = lax.rem(v + a, 2)
    return lax.rem(2 * w + p * (1 - 2 * c) + 8, 8)


def call(kernel, outs, *args, **more):
    return pl.pallas_call(
        kernel,
        out_shape=[jax.ShapeDtypeStruct(*o) for o in outs],
        in_specs=[VMEM] * len(args),
        out_specs=[VMEM] * len(outs),
        compiler_params=PARAMS,
        interpret=INTERPRET,
        **more,
    )(*args)


def first_kernel(me, tokens, master, moment, second, gradient, r0, r1, weight, out_master, out_moment, out_second, rows, sems):
    far = pl.multiple_of(2048 * (1 - me[3]), 2048)
    loads = [
        pltpu.make_async_copy(ref, rows.at[i], sems.at[i]) for i, ref in enumerate((master, moment, second, gradient))
    ]
    copies = [
        pltpu.make_async_copy(tokens.at[:, :, pl.ds(far + 4096 * i, 2048)], ref, sems.at[4 + i])
        for i, ref in enumerate((r0, r1))
    ]
    for copy in loads + copies:
        copy.start()
    for copy in loads:
        copy.wait()
    new_moment = 0.9 * rows[1] + 0.1 * rows[3]
    new_second = 0.95 * rows[2] + 0.05 * rows[3] * rows[3]
    first_fix = 1.0 - 0.9**10
    second_fix = 1.0 - 0.95**10
    update = new_moment / first_fix / (jnp.sqrt(new_second / second_fix) + 1e-08) + 0.1 * rows[0]
    new_master = rows[0] - 0.001 * update
    out_master[...] = new_master
    out_moment[...] = new_moment
    out_second[...] = new_second
    weight[...] = new_master.astype(BF16)
    for copy in copies:
        copy.wait()


def first(me, tokens, master, moment, second, gradient):
    half = jax.ShapeDtypeStruct((*tokens.shape[:2], 2048), BF16)
    rows = jax.ShapeDtypeStruct(master.shape, F32)
    return pl.pallas_call(
        first_kernel,
        in_specs=[SMEM] + [HBM] * 5,
        out_specs=[VMEM] * 6,
        out_shape=[half, half, jax.ShapeDtypeStruct(master.shape, BF16), rows, rows, rows],
        scratch_shapes=[pltpu.VMEM((4, *master.shape), F32), pltpu.SemaphoreType.DMA((6,))],
        compiler_params=PARAMS,
        interpret=INTERPRET,
    )(me, tokens, master, moment, second, gradient)


def terms_kernel(me, tokens, r0, r1, cot, cotr, sx, sy, sz, kx, ky, kz, own, sems):
    mx, my, mz, c = me[0], me[1], me[2], me[3]
    mine = pl.multiple_of(2048 * c, 2048)
    loads = [
        pltpu.make_async_copy(tokens.at[:, :, pl.ds(mine + 4096 * (t // 4) + 512 * (t % 4), 512)], own.at[t], sems.at[t])
        for t in range(8)
    ]
    for load in loads:
        load.start()
    flat = cot.shape[0] * cot.shape[1]
    ours, theirs = cot[...].reshape(flat, 512), cotr[...].reshape(flat, 512)
    xs = [label4(x, mx, c) for x in range(4)]
    ys = [label4(y, my, c) for y in range(4)]
    zs = [label8(z, mz, c) for z in range(8)]

    def product(a, b):
        return lax.dot_general(a.reshape(flat, 512), b, (((0,), (0,)), ((), ())), preferred_element_type=F32)

    for t in range(8):
        other = (r0, r1)[t // 4][:, :, 512 * (t % 4) : 512 * (t % 4) + 512]
        acc = product(other, theirs)
        loads[t].wait()
        acc += product(own[t], ours)
        for j in range(16):
            x, y, z = xs[t % 4], ys[2 * (t // 4) + j // 8], zs[j % 8]
            far = x[1] * 8 + y[1] * 4 + z[1]
            axes = (x[0], y[0], z[0])
            block = acc[32 * j : 32 * j + 32]
            for stream, (send, keep) in enumerate(((sx, kx), (sy, ky), (sz, kz))):
                first_, second_, third_ = (axes[axis] for axis in AXES[stream])
                at = second_ * 32 + third_ * 16 + far
                part = cut(stream, block)
                send[jnp.where(first_ == 1, at, 64)] = part.astype(BF16)
                keep[jnp.where(first_ == 1, 64, at)] = part


def all_terms(me, tokens, r0, r1, cot, cotr):
    return pl.pallas_call(
        terms_kernel,
        in_specs=[SMEM, HBM] + [VMEM] * 4,
        out_specs=[VMEM] * 6,
        out_shape=[jax.ShapeDtypeStruct(*message(65, i)) for i in range(3)]
        + [jax.ShapeDtypeStruct((65, *s), F32) for s in STREAMS],
        scratch_shapes=[pltpu.VMEM((8, *tokens.shape[:2], 512), BF16), pltpu.SemaphoreType.DMA((8,))],
        compiler_params=PARAMS,
        interpret=INTERPRET,
    )(me, tokens, r0, r1, cot, cotr)


def cut(stream, block):
    return (block[..., 0:16, 0:384], block[..., 16:32, 0:384], block[..., :, 384:512])[stream]


def second_kernel(stream, got, keep, plane, send, kept):
    send[0:32] = (keep[32:64] + got[32:64].astype(F32)).astype(BF16)
    send[32:48] = cut(stream, plane[...])
    kept[...] = keep[0:32] + got[0:32].astype(F32)


def third_kernel(got, keep, sent, send, kept):
    send[0:16] = (keep[16:32] + got[16:32].astype(F32)).astype(BF16)
    send[16:32] = sent[32:48]
    send[32:48] = got[32:48]
    kept[...] = keep[0:16] + got[0:16].astype(F32)


def fourth_kernel(got, sent, send):
    send[0:32] = sent[16:48]
    send[32:64] = got[16:48]


def far_kernel(gx, gy, gz, kx, ky, kz, s0, s1, k0, k1):
    for out, start, stride in ((s0, 8, 4), (k0, 0, 4), (s1, 6, 8), (k1, 2, 8)):
        for i in range(2):
            at, to = slice(start + stride * i, start + stride * i + 2), slice(2 * i, 2 * i + 2)
            out[to, 0:16, 0:384] = (kx[at] + gx[at].astype(F32)).astype(out.dtype)
            out[to, 16:32, 0:384] = (ky[at] + gy[at].astype(F32)).astype(out.dtype)
            out[to, :, 384:512] = (kz[at] + gz[at].astype(F32)).astype(out.dtype)


def across_kernel(g0, g1, k0, k1, s0, s1, kept):
    for i, (got, keep, send) in enumerate(((g0, k0, s0), (g1, k1, s1))):
        send[...] = (keep[2:4] + got[2:4].astype(F32)).astype(BF16)
        kept[2 * i : 2 * i + 2] = keep[0:2] + got[0:2].astype(F32)


def line_kernel(g0, g1, keep, send, kept):
    send[...] = (keep[2:4] + g1[...].astype(F32)).astype(BF16)
    kept[...] = keep[0:2] + g0[...].astype(F32)


def last_kernel(got, keep, send, kept):
    send[...] = (keep[1] + got[1].astype(F32)).astype(BF16)
    kept[...] = keep[0] + got[0].astype(F32)


def sum_kernel(got, keep, out):
    out[...] = keep[...] + got[...].astype(F32)


def assemble(me, sx, sy, sz, gx, gy, gz, w):
    mx, my, mz, c = me[0], me[1], me[2], me[3]
    xs = [[reached4(mx, c, a, b) * 512 for b in range(2)] for a in range(2)]
    ys = [[reached4(my, c, a, b) for b in range(2)] for a in range(2)]
    ys = [[(y // 2) * 2048 + lax.rem(y, 2) * 256 for y in row] for row in ys]
    zs = [[reached8(mz, c, a, d) * 32 for d in range(4)] for a in range(2)]
    for xa in range(2):
        for ya in range(2):
            for za in range(2):
                for i in range(16):
                    at = pl.multiple_of(xs[xa][i // 8] + ys[ya][(i // 4) % 2] + zs[za][i % 4], 32)
                    label = (xa, ya, za)

                    def part(stream, sent, got):
                        first, second, third = (label[axis] for axis in AXES[stream])
                        return (got if first else sent)[third * 32 + second * 16 + i]

                    w[pl.ds(at, 16), 0:384] = part(0, sx, gx)
                    w[pl.ds(at + 16, 16), 0:384] = part(1, sy, gy)
                    w[pl.ds(at, 32), 384:512] = part(2, sz, gz)


def other_kernel(me, tokens, r0, r1, sx, sy, sz, gx, gy, gz, out, w, own, sems):
    mine = pl.multiple_of(2048 * me[3], 2048)
    loads = [
        pltpu.make_async_copy(tokens.at[:, :, pl.ds(mine + 4096 * i, 2048)], own.at[i], sems.at[i]) for i in range(2)
    ]
    for load in loads:
        load.start()
    assemble(me, sx, sy, sz, gx, gy, gz, w)
    for m in range(out.shape[0]):
        out[m] = jnp.dot(r0[m], w[0:2048], preferred_element_type=F32) + jnp.dot(
            r1[m], w[2048:4096], preferred_element_type=F32
        )
    for load in loads:
        load.wait()


def mine_kernel(own, w, other, out):
    for m in range(out.shape[0]):
        total = (
            other[m]
            + jnp.dot(own[0, m], w[0:2048], preferred_element_type=F32)
            + jnp.dot(own[1, m], w[2048:4096], preferred_element_type=F32)
        )
        out[m] = total.astype(BF16)


def other_values(me, tokens, r0, r1, messages):
    return pl.pallas_call(
        other_kernel,
        in_specs=[SMEM, HBM] + [VMEM] * 8,
        out_specs=[VMEM] * 3,
        out_shape=[
            jax.ShapeDtypeStruct((*r0.shape[:2], 512), F32),
            jax.ShapeDtypeStruct((4096, 512), BF16),
            jax.ShapeDtypeStruct((2, *r0.shape), BF16),
        ],
        scratch_shapes=[pltpu.SemaphoreType.DMA((2,))],
        compiler_params=PARAMS,
        interpret=INTERPRET,
    )(me, tokens, r0, r1, *messages)


def after(value, *others):
    return lax.optimization_barrier((value, *others))[0]


def body(tokens, cotangent, master, moment, second, gradient):
    node, dp = lax.axis_index("node"), lax.axis_index("dp")
    me = jnp.stack([dp // 16, (node // 2) * 2 + (dp // 8) % 2, dp % 8, node % 2]).astype(jnp.int32)

    tokens, master, moment, second, gradient = (
        pltpu.with_memory_space_constraint(a, pltpu.HBM) for a in (tokens, master, moment, second, gradient)
    )
    r0, r1, weight, new_master, new_moment, new_second = first(me, tokens, master, moment, second, gradient)
    r0, r1, cotr = swap(r0), swap(r1), swap(cotangent)
    line = jnp.stack([weight, far_step(weight, 2, True)])
    line = jnp.concatenate([line, far_step(line, 2, False)])
    terms = all_terms(me, tokens, r0, r1, cotangent, cotr)
    send, keep = terms[:3], terms[3:]

    got = [near(send[i], AXES[i][0]) for i in range(3)]
    line = after(line, send[0])
    plane = jnp.concatenate([line, far_step(line, 1, False)])
    plane = jnp.concatenate([plane, far_step(plane, 0, False)])

    *got, plane = lax.optimization_barrier((*got, plane))
    new = [
        call(
            functools.partial(second_kernel, i),
            [message(48, i), ((32, *STREAMS[i]), F32)],
            got[i],
            keep[i],
            plane,
        )
        for i in range(3)
    ]
    send, keep = [n[0] for n in new], [n[1] for n in new]
    got = [near(send[i], AXES[i][1]) for i in range(3)]

    new = [
        call(third_kernel, [message(48, i), ((16, *STREAMS[i]), F32)], got[i], keep[i], send[i])
        for i in range(3)
    ]
    send, keep = [n[0] for n in new], [n[1] for n in new]
    got = [near(send[i], AXES[i][2]) for i in range(3)]

    block = (32, 512)
    s0, s1, k0, k1 = call(far_kernel, [((4, *block), BF16)] * 2 + [((4, *block), F32)] * 2, *got, *keep)
    half = [call(fourth_kernel, [message(64, i)], got[i], send[i])[0] for i in range(3)]
    g0, g1 = far_step(s0, 0, False), far_step(s1, 1, False)
    rest = [near(half[i], AXES[i][0]) for i in range(3)]
    s0, s1, kept = call(across_kernel, [((2, *block), BF16)] * 2 + [((4, *block), F32)], g0, g1, k0, k1)
    g0, g1 = far_step(s0, 1, False), far_step(s1, 0, False)
    s, kept = call(line_kernel, [((2, *block), BF16), ((2, *block), F32)], g0, g1, kept)
    got = far_step(s, 2, False)

    other, w, own = other_values(after(me, kept), tokens, r0, r1, [*half, *rest])
    s, kept = call(last_kernel, [(block, BF16), (block, F32)], got, after(kept, w))
    got = far_step(s, 2, True)
    (values,) = call(mine_kernel, [((*r0.shape[:2], 512), BF16)], own, w, swap(after(other, kept)))
    (weight_grad,) = call(sum_kernel, [(block, F32)], got, after(kept, values))
    return (new_master, new_moment, new_second, values, weight_grad)


def solution(mesh):
    rows = P(("node", "dp"), None)
    tall = P(None, ("node", "dp"), None)
    return jax.shard_map(
        body,
        mesh=mesh,
        in_specs=(tall, tall, rows, rows, rows, rows),
        out_specs=(rows, rows, rows, tall, rows),
        check_vma=False,
    )
```

```python
import functools
import jax
import jax.numpy as jnp
from jax import lax
from jax.experimental import pallas as pl
from jax.experimental.pallas import tpu as pltpu
from jax.sharding import PartitionSpec as P

F32, BF16 = jnp.float32, jnp.bfloat16
ALL = ("node", "dp")
INTERPRET = False
VMEM = pl.BlockSpec(memory_space=pltpu.VMEM)
SMEM = pl.BlockSpec(memory_space=pltpu.SMEM)
HBM = pl.BlockSpec(memory_space=pltpu.HBM)
PARAMS = pltpu.CompilerParams(vmem_limit_bytes=28 << 20)


STREAMS = ((16, 384), (16, 384), (32, 128))
AXES = ((0, 1, 2), (1, 2, 0), (2, 0, 1))


def message(n, stream):
    return (n + n // 2 if stream == 2 else n, *STREAMS[stream]), BF16


def place(x, y, z, c):
    return ((((y // 2) * 2 + c) * 4 + x) * 2 + y % 2) * 8 + z


def permute(value, move):
    pairs = []
    for c in range(2):
        for x in range(4):
            for y in range(4):
                for z in range(8):
                    pairs.append((place(x, y, z, c), place(*move(x, y, z, c))))
    return lax.ppermute(value, ALL, pairs)


def neighbour(v, n, c):
    return (v + 1 - 2 * ((v + c) % 2)) % n


def near(value, axis):
    def move(x, y, z, c):
        at = [x, y, z]
        at[axis] = neighbour(at[axis], (4, 4, 8)[axis], c)
        return (*at, c)

    return permute(value, move)


def far_step(value, axis, second):
    def move(x, y, z, c):
        at = [x, y, z]
        if axis < 2:
            at[axis] = neighbour(at[axis], 4, 1 - c)
        else:
            w = neighbour((z + c) // 2 % 4, 4, (1 - c) if second else c)
            at[2] = (2 * w + (z % 2) * (1 - 2 * c)) % 8
        return (*at, c)

    return permute(value, move)


def swap(value):
    return permute(value, lambda x, y, z, c: (x, y, z, 1 - c))


def as_int(flag):
    return jnp.where(flag, 1, 0)


def label4(u, v, c):
    step = 1 - 2 * lax.rem(v + c, 2)
    delta = lax.rem(u - v + 4, 4)
    far = delta == 2
    return as_int(far | (delta == lax.rem(step + 4, 4))), as_int(far | (delta == lax.rem(4 - step, 4)))


def label8(u, v, c):
    b, d = label4(lax.rem((u + c) // 2, 4), lax.rem((v + c) // 2, 4), c)
    return lax.rem(u + v, 2), b * 2 + d


def reached4(v, c, a, b):
    step = 1 - 2 * lax.rem(v + c, 2)
    return lax.rem(v + (2 if a and b else a * step - b * step) + 4, 4)


def reached8(v, c, a, d):
    w = reached4(lax.rem((v + c) // 2, 4), c, d // 2, d % 2)
    p = lax.rem(v + a, 2)
    return lax.rem(2 * w + p * (1 - 2 * c) + 8, 8)


def call(kernel, outs, *args, **more):
    return pl.pallas_call(
        kernel,
        out_shape=[jax.ShapeDtypeStruct(*o) for o in outs],
        in_specs=[VMEM] * len(args),
        out_specs=[VMEM] * len(outs),
        compiler_params=PARAMS,
        interpret=INTERPRET,
        **more,
    )(*args)


def load_half(tokens, column, to, sems, at):
    half = tokens.shape[1] // 2
    pieces = [(i, m, h) for i in range(2) for m in range(2) for h in range(2)]
    return [
        pltpu.make_async_copy(
            tokens.at[m, pl.ds(half * h, half), pl.ds(column + 4096 * i, 2048)],
            to[i].at[m, pl.ds(half * h, half)],
            sems.at[at + n],
        )
        for n, (i, m, h) in enumerate(pieces)
    ]


def first_kernel(me, tokens, master, moment, second, gradient, r0, r1, weight, out_master, out_moment, out_second, rows, sems):
    far = pl.multiple_of(2048 * (1 - me[3]), 2048)
    loads = [
        pltpu.make_async_copy(ref, rows.at[i], sems.at[i]) for i, ref in enumerate((master, moment, second, gradient))
    ]
    copies = load_half(tokens, far, (r0, r1), sems, 4)
    for copy in loads + copies:
        copy.start()
    for copy in loads:
        copy.wait()
    new_moment = 0.9 * rows[1] + 0.1 * rows[3]
    new_second = 0.95 * rows[2] + 0.05 * rows[3] * rows[3]
    first_fix = 1.0 - 0.9**10
    second_fix = 1.0 - 0.95**10
    update = new_moment / first_fix / (jnp.sqrt(new_second / second_fix) + 1e-08) + 0.1 * rows[0]
    new_master = rows[0] - 0.001 * update
    out_master[...] = new_master
    out_moment[...] = new_moment
    out_second[...] = new_second
    weight[...] = new_master.astype(BF16)
    for copy in copies:
        copy.wait()


def first(me, tokens, master, moment, second, gradient):
    half = jax.ShapeDtypeStruct((*tokens.shape[:2], 2048), BF16)
    rows = jax.ShapeDtypeStruct(master.shape, F32)
    return pl.pallas_call(
        first_kernel,
        in_specs=[SMEM] + [HBM] * 5,
        out_specs=[VMEM] * 6,
        out_shape=[half, half, jax.ShapeDtypeStruct(master.shape, BF16), rows, rows, rows],
        scratch_shapes=[pltpu.VMEM((4, *master.shape), F32), pltpu.SemaphoreType.DMA((12,))],
        compiler_params=PARAMS,
        interpret=INTERPRET,
    )(me, tokens, master, moment, second, gradient)


def terms_kernel(part, me, tokens, other, cot, cotr, *refs):
    sx, sy, sz, kx, ky, kz, own, sems = refs[-8:]
    mx, my, mz, c = me[0], me[1], me[2], me[3]
    mine = pl.multiple_of(2048 * c, 2048)
    loads = [
        pltpu.make_async_copy(tokens.at[:, :, pl.ds(mine + 4096 * part + 512 * x, 512)], own.at[x], sems.at[x])
        for x in range(4)
    ]
    for load in loads:
        load.start()
    flat = cot.shape[0] * cot.shape[1]
    ours, theirs = cot[...].reshape(flat, 512), cotr[...].reshape(flat, 512)
    xs = [label4(x, mx, c) for x in range(4)]
    ys = [label4(2 * part + y, my, c) for y in range(2)]
    zs = [label8(z, mz, c) for z in range(8)]

    def product(a, b):
        return lax.dot_general(a.reshape(flat, 512), b, (((0,), (0,)), ((), ())), preferred_element_type=F32)

    for t in range(4):
        acc = product(other[:, :, 512 * t : 512 * t + 512], theirs)
        loads[t].wait()
        acc += product(own[t], ours)
        for j in range(16):
            x, y, z = xs[t], ys[j // 8], zs[j % 8]
            far = x[1] * 8 + y[1] * 4 + z[1]
            axes = (x[0], y[0], z[0])
            block = acc[32 * j : 32 * j + 32]
            for stream, (send, keep) in enumerate(((sx, kx), (sy, ky), (sz, kz))):
                first_, second_, third_ = (axes[axis] for axis in AXES[stream])
                at = second_ * 32 + third_ * 16 + far
                piece = cut(stream, block)
                send[jnp.where(first_ == 1, at, 64)] = piece.astype(BF16)
                keep[jnp.where(first_ == 1, 64, at)] = piece


def terms(part, me, tokens, other, cot, cotr, held=()):
    return pl.pallas_call(
        functools.partial(terms_kernel, part),
        in_specs=[SMEM, HBM] + [VMEM] * (3 + len(held)),
        out_specs=[VMEM] * 6,
        out_shape=[jax.ShapeDtypeStruct(*message(65, i)) for i in range(3)]
        + [jax.ShapeDtypeStruct((65, *s), F32) for s in STREAMS],
        scratch_shapes=[pltpu.VMEM((4, *tokens.shape[:2], 512), BF16), pltpu.SemaphoreType.DMA((4,))],
        input_output_aliases={5 + i: i for i in range(len(held))},
        compiler_params=PARAMS,
        interpret=INTERPRET,
    )(me, tokens, other, cot, cotr, *held)


def cut(stream, block):
    return (block[..., 0:16, 0:384], block[..., 16:32, 0:384], block[..., :, 384:512])[stream]


def second_kernel(stream, got, keep, plane, send, kept):
    send[0:32] = (keep[32:64] + got[32:64].astype(F32)).astype(BF16)
    send[32:48] = cut(stream, plane[...])
    kept[...] = keep[0:32] + got[0:32].astype(F32)


def third_kernel(got, keep, sent, send, kept):
    send[0:16] = (keep[16:32] + got[16:32].astype(F32)).astype(BF16)
    send[16:32] = sent[32:48]
    send[32:48] = got[32:48]
    kept[...] = keep[0:16] + got[0:16].astype(F32)


def fourth_kernel(got, sent, send):
    send[0:32] = sent[16:48]
    send[32:64] = got[16:48]


def far_kernel(gx, gy, gz, kx, ky, kz, s0, s1, k0, k1):
    for out, start, stride in ((s0, 8, 4), (k0, 0, 4), (s1, 6, 8), (k1, 2, 8)):
        for i in range(2):
            at, to = slice(start + stride * i, start + stride * i + 2), slice(2 * i, 2 * i + 2)
            out[to, 0:16, 0:384] = (kx[at] + gx[at].astype(F32)).astype(out.dtype)
            out[to, 16:32, 0:384] = (ky[at] + gy[at].astype(F32)).astype(out.dtype)
            out[to, :, 384:512] = (kz[at] + gz[at].astype(F32)).astype(out.dtype)


def across_kernel(g0, g1, k0, k1, s0, s1, kept):
    for i, (got, keep, send) in enumerate(((g0, k0, s0), (g1, k1, s1))):
        send[...] = (keep[2:4] + got[2:4].astype(F32)).astype(BF16)
        kept[2 * i : 2 * i + 2] = keep[0:2] + got[0:2].astype(F32)


def line_kernel(g0, g1, keep, send, kept):
    send[...] = (keep[2:4] + g1[...].astype(F32)).astype(BF16)
    kept[...] = keep[0:2] + g0[...].astype(F32)


def last_kernel(got, keep, send, kept):
    send[...] = (keep[1] + got[1].astype(F32)).astype(BF16)
    kept[...] = keep[0] + got[0].astype(F32)


def sum_kernel(got, keep, out):
    out[...] = keep[...] + got[...].astype(F32)


def assemble(me, sx, sy, sz, gx, gy, gz, w):
    mx, my, mz, c = me[0], me[1], me[2], me[3]
    xs = [[reached4(mx, c, a, b) * 512 for b in range(2)] for a in range(2)]
    ys = [[reached4(my, c, a, b) for b in range(2)] for a in range(2)]
    ys = [[(y // 2) * 2048 + lax.rem(y, 2) * 256 for y in row] for row in ys]
    zs = [[reached8(mz, c, a, d) * 32 for d in range(4)] for a in range(2)]
    for xa in range(2):
        for ya in range(2):
            for za in range(2):
                for i in range(16):
                    at = pl.multiple_of(xs[xa][i // 8] + ys[ya][(i // 4) % 2] + zs[za][i % 4], 32)
                    label = (xa, ya, za)

                    def part(stream, sent, got):
                        first, second, third = (label[axis] for axis in AXES[stream])
                        return (got if first else sent)[third * 32 + second * 16 + i]

                    w[pl.ds(at, 16), 0:384] = part(0, sx, gx)
                    w[pl.ds(at + 16, 16), 0:384] = part(1, sy, gy)
                    w[pl.ds(at, 32), 384:512] = part(2, sz, gz)


def other_kernel(me, tokens, r0, r1, sx, sy, sz, gx, gy, gz, out, w, own, sems):
    mine = pl.multiple_of(2048 * me[3], 2048)
    loads = load_half(tokens, mine, (own.at[0], own.at[1]), sems, 0)
    for load in loads:
        load.start()
    assemble(me, sx, sy, sz, gx, gy, gz, w)
    for m in range(out.shape[0]):
        out[m] = jnp.dot(r0[m], w[0:2048], preferred_element_type=F32) + jnp.dot(
            r1[m], w[2048:4096], preferred_element_type=F32
        )
    for load in loads:
        load.wait()


def mine_kernel(own, w, out):
    for m in range(out.shape[0]):
        out[m] = jnp.dot(own[0, m], w[0:2048], preferred_element_type=F32) + jnp.dot(
            own[1, m], w[2048:4096], preferred_element_type=F32
        )


def add_kernel(mine, other, out):
    out[...] = (mine[...] + other[...]).astype(BF16)


def other_values(me, tokens, r0, r1, messages):
    return pl.pallas_call(
        other_kernel,
        in_specs=[SMEM, HBM] + [VMEM] * 8,
        out_specs=[VMEM] * 3,
        out_shape=[
            jax.ShapeDtypeStruct((*r0.shape[:2], 512), F32),
            jax.ShapeDtypeStruct((4096, 512), BF16),
            jax.ShapeDtypeStruct((2, *r0.shape), BF16),
        ],
        scratch_shapes=[pltpu.SemaphoreType.DMA((8,))],
        compiler_params=PARAMS,
        interpret=INTERPRET,
    )(me, tokens, r0, r1, *messages)


def after(value, *others):
    return lax.optimization_barrier((value, *others))[0]


def joined(a, b, other):
    return jnp.concatenate(lax.optimization_barrier((a, b, other))[:2])


def body(tokens, cotangent, master, moment, second, gradient):
    node, dp = lax.axis_index("node"), lax.axis_index("dp")
    me = jnp.stack([dp // 16, (node // 2) * 2 + (dp // 8) % 2, dp % 8, node % 2]).astype(jnp.int32)

    tokens, master, moment, second, gradient = (
        pltpu.with_memory_space_constraint(a, pltpu.HBM) for a in (tokens, master, moment, second, gradient)
    )
    r0, r1, weight, new_master, new_moment, new_second = first(me, tokens, master, moment, second, gradient)
    cotr, r0, r1 = swap(cotangent), swap(r0), swap(r1)
    line = jnp.stack([weight, far_step(weight, 2, True)])
    held = terms(0, me, tokens, r0, cotangent, cotr)
    line = joined(line, far_step(line, 2, False), held[0])
    far = far_step(line, 1, False)
    held = terms(1, me, tokens, r1, cotangent, cotr, held)
    send, keep = held[:3], held[3:]
    plane = joined(line, far, send[0])
    plane = jnp.concatenate([plane, far_step(plane, 0, False)])
    got = [near(send[i], AXES[i][0]) for i in range(3)]

    *got, plane = lax.optimization_barrier((*got, plane))
    new = [
        call(
            functools.partial(second_kernel, i),
            [message(48, i), ((32, *STREAMS[i]), F32)],
            got[i],
            keep[i],
            plane,
        )
        for i in range(3)
    ]
    send, keep = [n[0] for n in new], [n[1] for n in new]
    got = [near(send[i], AXES[i][1]) for i in range(3)]

    new = [
        call(third_kernel, [message(48, i), ((16, *STREAMS[i]), F32)], got[i], keep[i], send[i])
        for i in range(3)
    ]
    send, keep = [n[0] for n in new], [n[1] for n in new]
    got = [near(send[i], AXES[i][2]) for i in range(3)]

    block = (32, 512)
    s0, s1, k0, k1 = call(far_kernel, [((4, *block), BF16)] * 2 + [((4, *block), F32)] * 2, *got, *keep)
    g0, g1 = far_step(s0, 0, False), far_step(s1, 1, False)
    half = [call(fourth_kernel, [message(64, i)], got[i], send[i])[0] for i in range(3)]
    rest = [near(half[i], AXES[i][0]) for i in range(3)]
    s0, s1, kept = call(across_kernel, [((2, *block), BF16)] * 2 + [((4, *block), F32)], g0, g1, k0, k1)
    g0, g1 = far_step(s0, 1, False), far_step(s1, 0, False)
    s, kept = call(line_kernel, [((2, *block), BF16), ((2, *block), F32)], g0, g1, kept)
    got = far_step(s, 2, False)

    other, w, own = other_values(after(me, kept), tokens, r0, r1, [*half, *rest])
    s, kept = call(last_kernel, [(block, BF16), (block, F32)], got, after(kept, w))
    got = far_step(s, 2, True)
    other = swap(after(other, kept))
    (mine,) = call(mine_kernel, [((*r0.shape[:2], 512), F32)], own, after(w, kept))
    (weight_grad,) = call(sum_kernel, [(block, F32)], got, after(kept, mine))
    (values,) = call(add_kernel, [((*r0.shape[:2], 512), BF16)], mine, other)
    return (new_master, new_moment, new_second, values, weight_grad)


def solution(mesh):
    rows = P(("node", "dp"), None)
    tall = P(None, ("node", "dp"), None)
    return jax.shard_map(
        body,
        mesh=mesh,
        in_specs=(tall, tall, rows, rows, rows, rows),
        out_specs=(rows, rows, rows, tall, rows),
        check_vma=False,
    )
```

```python
import functools
import jax
import jax.numpy as jnp
from jax import lax
from jax.experimental import pallas as pl
from jax.experimental.pallas import tpu as pltpu
from jax.sharding import PartitionSpec as P

F32, BF16 = jnp.float32, jnp.bfloat16
ALL = ("node", "dp")
INTERPRET = False
VMEM = pl.BlockSpec(memory_space=pltpu.VMEM)
SMEM = pl.BlockSpec(memory_space=pltpu.SMEM)
HBM = pl.BlockSpec(memory_space=pltpu.HBM)
PARAMS = pltpu.CompilerParams(vmem_limit_bytes=28 << 20)


STREAMS = ((16, 384), (16, 384), (32, 128))
AXES = ((0, 1, 2), (1, 2, 0), (2, 0, 1))


def message(n, stream):
    return (n + n // 2 if stream == 2 else n, *STREAMS[stream]), BF16


def place(x, y, z, c):
    return ((((y // 2) * 2 + c) * 4 + x) * 2 + y % 2) * 8 + z


def permute(value, move):
    pairs = []
    for c in range(2):
        for x in range(4):
            for y in range(4):
                for z in range(8):
                    pairs.append((place(x, y, z, c), place(*move(x, y, z, c))))
    return lax.ppermute(value, ALL, pairs)


def neighbour(v, n, c):
    return (v + 1 - 2 * ((v + c) % 2)) % n


def near(value, axis):
    def move(x, y, z, c):
        at = [x, y, z]
        at[axis] = neighbour(at[axis], (4, 4, 8)[axis], c)
        return (*at, c)

    return permute(value, move)


def far_step(value, axis, second):
    def move(x, y, z, c):
        at = [x, y, z]
        if axis < 2:
            at[axis] = neighbour(at[axis], 4, 1 - c)
        else:
            w = neighbour((z + c) // 2 % 4, 4, (1 - c) if second else c)
            at[2] = (2 * w + (z % 2) * (1 - 2 * c)) % 8
        return (*at, c)

    return permute(value, move)


def swap(value):
    return permute(value, lambda x, y, z, c: (x, y, z, 1 - c))


def as_int(flag):
    return jnp.where(flag, 1, 0)


def label4(u, v, c):
    step = 1 - 2 * lax.rem(v + c, 2)
    delta = lax.rem(u - v + 4, 4)
    far = delta == 2
    return as_int(far | (delta == lax.rem(step + 4, 4))), as_int(far | (delta == lax.rem(4 - step, 4)))


def label8(u, v, c):
    b, d = label4(lax.rem((u + c) // 2, 4), lax.rem((v + c) // 2, 4), c)
    return lax.rem(u + v, 2), b * 2 + d


def reached4(v, c, a, b):
    step = 1 - 2 * lax.rem(v + c, 2)
    return lax.rem(v + (2 if a and b else a * step - b * step) + 4, 4)


def reached8(v, c, a, d):
    w = reached4(lax.rem((v + c) // 2, 4), c, d // 2, d % 2)
    p = lax.rem(v + a, 2)
    return lax.rem(2 * w + p * (1 - 2 * c) + 8, 8)


def call(kernel, outs, *args, **more):
    return pl.pallas_call(
        kernel,
        out_shape=[jax.ShapeDtypeStruct(*o) for o in outs],
        in_specs=[VMEM] * len(args),
        out_specs=[VMEM] * len(outs),
        compiler_params=PARAMS,
        interpret=INTERPRET,
        **more,
    )(*args)


def load_half(tokens, column, to, sems, at):
    half = tokens.shape[1] // 2
    pieces = [(i, m, h) for i in range(2) for m in range(2) for h in range(2)]
    return [
        pltpu.make_async_copy(
            tokens.at[m, pl.ds(half * h, half), pl.ds(column + 4096 * i, 2048)],
            to[i].at[m, pl.ds(half * h, half)],
            sems.at[at + n],
        )
        for n, (i, m, h) in enumerate(pieces)
    ]


def first_kernel(me, tokens, master, moment, second, gradient, r0, r1, weight, out_master, out_moment, out_second, rows, sems):
    far = pl.multiple_of(2048 * (1 - me[3]), 2048)
    loads = [
        pltpu.make_async_copy(ref, rows.at[i], sems.at[i]) for i, ref in enumerate((master, moment, second, gradient))
    ]
    copies = load_half(tokens, far, (r0, r1), sems, 4)
    for copy in loads + copies:
        copy.start()
    for copy in loads:
        copy.wait()
    new_moment = 0.9 * rows[1] + 0.1 * rows[3]
    new_second = 0.95 * rows[2] + 0.05 * rows[3] * rows[3]
    first_fix = 1.0 - 0.9**10
    second_fix = 1.0 - 0.95**10
    update = new_moment / first_fix / (jnp.sqrt(new_second / second_fix) + 1e-08) + 0.1 * rows[0]
    new_master = rows[0] - 0.001 * update
    out_master[...] = new_master
    out_moment[...] = new_moment
    out_second[...] = new_second
    weight[...] = new_master.astype(BF16)
    for copy in copies:
        copy.wait()


def first(me, tokens, master, moment, second, gradient):
    half = jax.ShapeDtypeStruct((*tokens.shape[:2], 2048), BF16)
    rows = jax.ShapeDtypeStruct(master.shape, F32)
    return pl.pallas_call(
        first_kernel,
        in_specs=[SMEM] + [HBM] * 5,
        out_specs=[VMEM] * 6,
        out_shape=[half, half, jax.ShapeDtypeStruct(master.shape, BF16), rows, rows, rows],
        scratch_shapes=[pltpu.VMEM((4, *master.shape), F32), pltpu.SemaphoreType.DMA((12,))],
        compiler_params=PARAMS,
        interpret=INTERPRET,
    )(me, tokens, master, moment, second, gradient)


def product(a, b):
    flat = b.shape[0] * b.shape[1]
    return lax.dot_general(
        a.reshape(flat, 512), b[...].reshape(flat, 512), (((0,), (0,)), ((), ())), preferred_element_type=F32
    )


def own_kernel(me, tokens, cot, out, own, sems):
    column = pl.multiple_of(2048 * me[3], 2048)
    loads = [
        pltpu.make_async_copy(
            tokens.at[:, :, pl.ds(column + 4096 * (t // 4) + 512 * (t % 4), 512)], own.at[t], sems.at[t]
        )
        for t in range(8)
    ]
    for load in loads:
        load.start()
    for t in range(8):
        loads[t].wait()
        out[t] = product(own[t], cot)


def own_terms(me, tokens, cot):
    return pl.pallas_call(
        own_kernel,
        in_specs=[SMEM, HBM, VMEM],
        out_specs=[VMEM] * 2,
        out_shape=[
            jax.ShapeDtypeStruct((8, 512, 512), F32),
            jax.ShapeDtypeStruct((8, *tokens.shape[:2], 512), BF16),
        ],
        scratch_shapes=[pltpu.SemaphoreType.DMA((8,))],
        compiler_params=PARAMS,
        interpret=INTERPRET,
    )(me, tokens, cot)


def terms_kernel(me, r0, r1, cot, mine, sx, sy, sz, kx, ky, kz):
    mx, my, mz, c = me[0], me[1], me[2], me[3]
    xs = [label4(x, mx, c) for x in range(4)]
    ys = [label4(y, my, c) for y in range(4)]
    zs = [label8(z, mz, c) for z in range(8)]
    for t in range(8):
        acc = mine[t] + product((r0, r1)[t // 4][:, :, 512 * (t % 4) : 512 * (t % 4) + 512], cot)
        for j in range(16):
            x, y, z = xs[t % 4], ys[2 * (t // 4) + j // 8], zs[j % 8]
            far = x[1] * 8 + y[1] * 4 + z[1]
            axes = (x[0], y[0], z[0])
            block = acc[32 * j : 32 * j + 32]
            for stream, (send, keep) in enumerate(((sx, kx), (sy, ky), (sz, kz))):
                first_, second_, third_ = (axes[axis] for axis in AXES[stream])
                at = second_ * 32 + third_ * 16 + far
                piece = cut(stream, block)
                send[jnp.where(first_ == 1, at, 64)] = piece.astype(BF16)
                keep[jnp.where(first_ == 1, 64, at)] = piece


def all_terms(me, r0, r1, cot, mine):
    return pl.pallas_call(
        terms_kernel,
        in_specs=[SMEM] + [VMEM] * 4,
        out_specs=[VMEM] * 6,
        out_shape=[jax.ShapeDtypeStruct(*message(65, i)) for i in range(3)]
        + [jax.ShapeDtypeStruct((65, *s), F32) for s in STREAMS],
        compiler_params=PARAMS,
        interpret=INTERPRET,
    )(me, r0, r1, cot, mine)


def cut(stream, block):
    return (block[..., 0:16, 0:384], block[..., 16:32, 0:384], block[..., :, 384:512])[stream]


def second_kernel(stream, got, keep, plane, send, kept):
    send[0:32] = (keep[32:64] + got[32:64].astype(F32)).astype(BF16)
    send[32:48] = cut(stream, plane[...])
    kept[...] = keep[0:32] + got[0:32].astype(F32)


def third_kernel(got, keep, sent, send, kept):
    send[0:16] = (keep[16:32] + got[16:32].astype(F32)).astype(BF16)
    send[16:32] = sent[32:48]
    send[32:48] = got[32:48]
    kept[...] = keep[0:16] + got[0:16].astype(F32)


def fourth_kernel(got, sent, send):
    send[0:32] = sent[16:48]
    send[32:64] = got[16:48]


def far_kernel(gx, gy, gz, kx, ky, kz, s0, s1, k0, k1):
    for out, start, stride in ((s0, 8, 4), (k0, 0, 4), (s1, 6, 8), (k1, 2, 8)):
        for i in range(2):
            at, to = slice(start + stride * i, start + stride * i + 2), slice(2 * i, 2 * i + 2)
            out[to, 0:16, 0:384] = (kx[at] + gx[at].astype(F32)).astype(out.dtype)
            out[to, 16:32, 0:384] = (ky[at] + gy[at].astype(F32)).astype(out.dtype)
            out[to, :, 384:512] = (kz[at] + gz[at].astype(F32)).astype(out.dtype)


def across_kernel(g0, g1, k0, k1, s0, s1, kept):
    for i, (got, keep, send) in enumerate(((g0, k0, s0), (g1, k1, s1))):
        send[...] = (keep[2:4] + got[2:4].astype(F32)).astype(BF16)
        kept[2 * i : 2 * i + 2] = keep[0:2] + got[0:2].astype(F32)


def line_kernel(g0, g1, keep, send, kept):
    send[...] = (keep[2:4] + g1[...].astype(F32)).astype(BF16)
    kept[...] = keep[0:2] + g0[...].astype(F32)


def last_kernel(got, keep, send, kept):
    send[...] = (keep[1] + got[1].astype(F32)).astype(BF16)
    kept[...] = keep[0] + got[0].astype(F32)


def assemble(me, sx, sy, sz, gx, gy, gz, w):
    mx, my, mz, c = me[0], me[1], me[2], me[3]
    xs = [[reached4(mx, c, a, b) * 512 for b in range(2)] for a in range(2)]
    ys = [[reached4(my, c, a, b) for b in range(2)] for a in range(2)]
    ys = [[(y // 2) * 2048 + lax.rem(y, 2) * 256 for y in row] for row in ys]
    zs = [[reached8(mz, c, a, d) * 32 for d in range(4)] for a in range(2)]
    for xa in range(2):
        for ya in range(2):
            for za in range(2):
                for i in range(16):
                    at = pl.multiple_of(xs[xa][i // 8] + ys[ya][(i // 4) % 2] + zs[za][i % 4], 32)
                    label = (xa, ya, za)

                    def part(stream, sent, got):
                        first, second, third = (label[axis] for axis in AXES[stream])
                        return (got if first else sent)[third * 32 + second * 16 + i]

                    w[pl.ds(at, 16), 0:384] = part(0, sx, gx)
                    w[pl.ds(at + 16, 16), 0:384] = part(1, sy, gy)
                    w[pl.ds(at, 32), 384:512] = part(2, sz, gz)


def other_kernel(me, r0, r1, sx, sy, sz, gx, gy, gz, out, w):
    assemble(me, sx, sy, sz, gx, gy, gz, w)
    for m in range(out.shape[0]):
        out[m] = jnp.dot(r0[m], w[0:2048], preferred_element_type=F32) + jnp.dot(
            r1[m], w[2048:4096], preferred_element_type=F32
        )


def mine_kernel(own, w, out):
    flat = out.shape[0] * out.shape[1]
    total = jnp.dot(own[0].reshape(flat, 512), w[0:512], preferred_element_type=F32)
    for t in range(1, 8):
        total += jnp.dot(own[t].reshape(flat, 512), w[512 * t : 512 * t + 512], preferred_element_type=F32)
    out[...] = total.reshape(out.shape)


def end_kernel(got, keep, mine, other, grad, values):
    grad[...] = keep[...] + got[...].astype(F32)
    values[...] = (mine[...] + other[...]).astype(BF16)


def other_values(me, r0, r1, messages):
    return pl.pallas_call(
        other_kernel,
        in_specs=[SMEM] + [VMEM] * 8,
        out_specs=[VMEM] * 2,
        out_shape=[
            jax.ShapeDtypeStruct((*r0.shape[:2], 512), F32),
            jax.ShapeDtypeStruct((4096, 512), BF16),
        ],
        compiler_params=PARAMS,
        interpret=INTERPRET,
    )(me, r0, r1, *messages)


def after(value, *others):
    return lax.optimization_barrier((value, *others))[0]


def body(tokens, cotangent, master, moment, second, gradient):
    node, dp = lax.axis_index("node"), lax.axis_index("dp")
    me = jnp.stack([dp // 16, (node // 2) * 2 + (dp // 8) % 2, dp % 8, node % 2]).astype(jnp.int32)

    tokens, master, moment, second, gradient = (
        pltpu.with_memory_space_constraint(a, pltpu.HBM) for a in (tokens, master, moment, second, gradient)
    )
    r0, r1, weight, new_master, new_moment, new_second = first(me, tokens, master, moment, second, gradient)
    cotr, r0, r1 = swap(cotangent), swap(r0), swap(r1)
    far = far_step(weight, 2, True)
    mine, own = own_terms(me, tokens, cotangent)
    line = jnp.stack(lax.optimization_barrier((weight, far, mine))[:2])
    line = jnp.concatenate([line, far_step(line, 2, False)])
    held = all_terms(me, r0, r1, cotr, mine)
    send, keep = held[:3], held[3:]

    got = [near(send[i], AXES[i][0]) for i in range(3)]
    line = after(line, send[0])
    plane = jnp.concatenate([line, far_step(line, 1, False)])
    plane = jnp.concatenate([plane, far_step(plane, 0, False)])

    *got, plane = lax.optimization_barrier((*got, plane))
    new = [
        call(
            functools.partial(second_kernel, i),
            [message(48, i), ((32, *STREAMS[i]), F32)],
            got[i],
            keep[i],
            plane,
        )
        for i in range(3)
    ]
    send, keep = [n[0] for n in new], [n[1] for n in new]
    got = [near(send[i], AXES[i][1]) for i in range(3)]

    new = [
        call(third_kernel, [message(48, i), ((16, *STREAMS[i]), F32)], got[i], keep[i], send[i])
        for i in range(3)
    ]
    send, keep = [n[0] for n in new], [n[1] for n in new]
    got = [near(send[i], AXES[i][2]) for i in range(3)]

    block = (32, 512)
    s0, s1, k0, k1 = call(far_kernel, [((4, *block), BF16)] * 2 + [((4, *block), F32)] * 2, *got, *keep)
    g0, g1 = far_step(s0, 0, False), far_step(s1, 1, False)
    half = [call(fourth_kernel, [message(64, i)], got[i], send[i])[0] for i in range(3)]
    rest = [near(half[i], AXES[i][0]) for i in range(3)]
    s0, s1, kept = call(across_kernel, [((2, *block), BF16)] * 2 + [((4, *block), F32)], g0, g1, k0, k1)
    g0, g1 = far_step(s0, 1, False), far_step(s1, 0, False)
    s, kept = call(line_kernel, [((2, *block), BF16), ((2, *block), F32)], g0, g1, kept)
    got = far_step(s, 2, False)

    other, w = other_values(after(me, kept), r0, r1, [*half, *rest])
    s, kept = call(last_kernel, [(block, BF16), (block, F32)], got, after(kept, w))
    got = far_step(s, 2, True)
    other = swap(after(other, kept))
    (mine,) = call(mine_kernel, [((*r0.shape[:2], 512), F32)], own, after(w, kept))
    weight_grad, values = call(
        end_kernel, [(block, F32), ((*r0.shape[:2], 512), BF16)], got, kept, mine, other
    )
    return (new_master, new_moment, new_second, values, weight_grad)


def solution(mesh):
    rows = P(("node", "dp"), None)
    tall = P(None, ("node", "dp"), None)
    return jax.shard_map(
        body,
        mesh=mesh,
        in_specs=(tall, tall, rows, rows, rows, rows),
        out_specs=(rows, rows, rows, tall, rows),
        check_vma=False,
    )
```

```python
import functools
import jax
import jax.numpy as jnp
from jax import lax
from jax.experimental import pallas as pl
from jax.experimental.pallas import tpu as pltpu
from jax.sharding import PartitionSpec as P

F32, BF16 = jnp.float32, jnp.bfloat16
ALL = ("node", "dp")
INTERPRET = False
VMEM = pl.BlockSpec(memory_space=pltpu.VMEM)
SMEM = pl.BlockSpec(memory_space=pltpu.SMEM)
HBM = pl.BlockSpec(memory_space=pltpu.HBM)
PARAMS = pltpu.CompilerParams(vmem_limit_bytes=28 << 20)


STREAMS = ((16, 384), (16, 384), (32, 128))
AXES = ((0, 1, 2), (1, 2, 0), (2, 0, 1))


def message(n, stream):
    return (n + n // 2 if stream == 2 else n, *STREAMS[stream]), BF16


def place(x, y, z, c):
    return ((((y // 2) * 2 + c) * 4 + x) * 2 + y % 2) * 8 + z


def permute(value, move):
    pairs = []
    for c in range(2):
        for x in range(4):
            for y in range(4):
                for z in range(8):
                    pairs.append((place(x, y, z, c), place(*move(x, y, z, c))))
    return lax.ppermute(value, ALL, pairs)


def neighbour(v, n, c):
    return (v + 1 - 2 * ((v + c) % 2)) % n


def near(value, axis):
    def move(x, y, z, c):
        at = [x, y, z]
        at[axis] = neighbour(at[axis], (4, 4, 8)[axis], c)
        return (*at, c)

    return permute(value, move)


def far_step(value, axis, second):
    def move(x, y, z, c):
        at = [x, y, z]
        if axis < 2:
            at[axis] = neighbour(at[axis], 4, 1 - c)
        else:
            w = neighbour((z + c) // 2 % 4, 4, (1 - c) if second else c)
            at[2] = (2 * w + (z % 2) * (1 - 2 * c)) % 8
        return (*at, c)

    return permute(value, move)


def swap(value):
    return permute(value, lambda x, y, z, c: (x, y, z, 1 - c))


def as_int(flag):
    return jnp.where(flag, 1, 0)


def label4(u, v, c):
    step = 1 - 2 * lax.rem(v + c, 2)
    delta = lax.rem(u - v + 4, 4)
    far = delta == 2
    return as_int(far | (delta == lax.rem(step + 4, 4))), as_int(far | (delta == lax.rem(4 - step, 4)))


def label8(u, v, c):
    b, d = label4(lax.rem((u + c) // 2, 4), lax.rem((v + c) // 2, 4), c)
    return lax.rem(u + v, 2), b * 2 + d


def reached4(v, c, a, b):
    step = 1 - 2 * lax.rem(v + c, 2)
    return lax.rem(v + (2 if a and b else a * step - b * step) + 4, 4)


def reached8(v, c, a, d):
    w = reached4(lax.rem((v + c) // 2, 4), c, d // 2, d % 2)
    p = lax.rem(v + a, 2)
    return lax.rem(2 * w + p * (1 - 2 * c) + 8, 8)


def call(kernel, outs, *args, **more):
    return pl.pallas_call(
        kernel,
        out_shape=[jax.ShapeDtypeStruct(*o) for o in outs],
        in_specs=[VMEM] * len(args),
        out_specs=[VMEM] * len(outs),
        compiler_params=PARAMS,
        interpret=INTERPRET,
        **more,
    )(*args)


def load_half(tokens, column, to, sems, at):
    half = tokens.shape[1] // 2
    pieces = [(i, m, h) for i in range(2) for m in range(2) for h in range(2)]
    return [
        pltpu.make_async_copy(
            tokens.at[m, pl.ds(half * h, half), pl.ds(column + 4096 * i, 2048)],
            to[i].at[m, pl.ds(half * h, half)],
            sems.at[at + n],
        )
        for n, (i, m, h) in enumerate(pieces)
    ]


def first_kernel(me, tokens, cot, master, moment, second, gradient, r0, r1, held, weight, out_master, out_moment, out_second, rows, sems):
    far = pl.multiple_of(2048 * (1 - me[3]), 2048)
    loads = [
        pltpu.make_async_copy(ref, rows.at[i], sems.at[i]) for i, ref in enumerate((master, moment, second, gradient))
    ]
    copies = load_half(tokens, far, (r0, r1), sems, 4)
    copies.append(pltpu.make_async_copy(cot, held, sems.at[12]))
    for copy in loads + copies:
        copy.start()
    for copy in loads:
        copy.wait()
    new_moment = 0.9 * rows[1] + 0.1 * rows[3]
    new_second = 0.95 * rows[2] + 0.05 * rows[3] * rows[3]
    first_fix = 1.0 - 0.9**10
    second_fix = 1.0 - 0.95**10
    update = new_moment / first_fix / (jnp.sqrt(new_second / second_fix) + 1e-08) + 0.1 * rows[0]
    new_master = rows[0] - 0.001 * update
    out_master[...] = new_master
    out_moment[...] = new_moment
    out_second[...] = new_second
    weight[...] = new_master.astype(BF16)
    for copy in copies:
        copy.wait()


def first(me, tokens, cot, master, moment, second, gradient):
    half = jax.ShapeDtypeStruct((*tokens.shape[:2], 2048), BF16)
    rows = jax.ShapeDtypeStruct(master.shape, F32)
    return pl.pallas_call(
        first_kernel,
        in_specs=[SMEM] + [HBM] * 6,
        out_specs=[VMEM] * 7,
        out_shape=[half, half, jax.ShapeDtypeStruct(cot.shape, BF16), jax.ShapeDtypeStruct(master.shape, BF16), rows, rows, rows],
        scratch_shapes=[pltpu.VMEM((4, *master.shape), F32), pltpu.SemaphoreType.DMA((13,))],
        compiler_params=PARAMS,
        interpret=INTERPRET,
    )(me, tokens, cot, master, moment, second, gradient)


def product(a, b):
    flat = b.shape[0] * b.shape[1]
    return lax.dot_general(
        a.reshape(flat, 512), b[...].reshape(flat, 512), (((0,), (0,)), ((), ())), preferred_element_type=F32
    )


def own_kernel(me, tokens, cot, out):
    for t in range(8):
        column = pl.multiple_of(2048 * me[3] + 4096 * (t // 4) + 512 * (t % 4), 512)
        out[t] = product(tokens[:, :, pl.ds(column, 512)], cot)


def own_terms(me, tokens, cot):
    return pl.pallas_call(
        own_kernel,
        in_specs=[SMEM, VMEM, VMEM],
        out_specs=VMEM,
        out_shape=jax.ShapeDtypeStruct((8, 512, 512), F32),
        compiler_params=PARAMS,
        interpret=INTERPRET,
    )(me, tokens, cot)


def terms_kernel(me, r0, r1, cot, mine, sx, sy, sz, kx, ky, kz):
    mx, my, mz, c = me[0], me[1], me[2], me[3]
    xs = [label4(x, mx, c) for x in range(4)]
    ys = [label4(y, my, c) for y in range(4)]
    zs = [label8(z, mz, c) for z in range(8)]
    for t in range(8):
        acc = mine[t] + product((r0, r1)[t // 4][:, :, 512 * (t % 4) : 512 * (t % 4) + 512], cot)
        for j in range(16):
            x, y, z = xs[t % 4], ys[2 * (t // 4) + j // 8], zs[j % 8]
            far = x[1] * 8 + y[1] * 4 + z[1]
            axes = (x[0], y[0], z[0])
            block = acc[32 * j : 32 * j + 32]
            for stream, (send, keep) in enumerate(((sx, kx), (sy, ky), (sz, kz))):
                first_, second_, third_ = (axes[axis] for axis in AXES[stream])
                at = second_ * 32 + third_ * 16 + far
                piece = cut(stream, block)
                send[jnp.where(first_ == 1, at, 64)] = piece.astype(BF16)
                keep[jnp.where(first_ == 1, 64, at)] = piece


def all_terms(me, r0, r1, cot, mine):
    return pl.pallas_call(
        terms_kernel,
        in_specs=[SMEM] + [VMEM] * 4,
        out_specs=[VMEM] * 6,
        out_shape=[jax.ShapeDtypeStruct(*message(65, i)) for i in range(3)]
        + [jax.ShapeDtypeStruct((65, *s), F32) for s in STREAMS],
        compiler_params=PARAMS,
        interpret=INTERPRET,
    )(me, r0, r1, cot, mine)


def cut(stream, block):
    return (block[..., 0:16, 0:384], block[..., 16:32, 0:384], block[..., :, 384:512])[stream]


def second_kernel(stream, got, keep, plane, send, kept):
    send[0:32] = (keep[32:64] + got[32:64].astype(F32)).astype(BF16)
    send[32:48] = cut(stream, plane[...])
    kept[...] = keep[0:32] + got[0:32].astype(F32)


def third_kernel(got, keep, sent, send, kept):
    send[0:16] = (keep[16:32] + got[16:32].astype(F32)).astype(BF16)
    send[16:32] = sent[32:48]
    send[32:48] = got[32:48]
    kept[...] = keep[0:16] + got[0:16].astype(F32)


def fourth_kernel(got, sent, send):
    send[0:32] = sent[16:48]
    send[32:64] = got[16:48]


def far_kernel(gx, gy, gz, kx, ky, kz, s0, s1, k0, k1):
    for out, start, stride in ((s0, 8, 4), (k0, 0, 4), (s1, 6, 8), (k1, 2, 8)):
        for i in range(2):
            at, to = slice(start + stride * i, start + stride * i + 2), slice(2 * i, 2 * i + 2)
            out[to, 0:16, 0:384] = (kx[at] + gx[at].astype(F32)).astype(out.dtype)
            out[to, 16:32, 0:384] = (ky[at] + gy[at].astype(F32)).astype(out.dtype)
            out[to, :, 384:512] = (kz[at] + gz[at].astype(F32)).astype(out.dtype)


def across_kernel(g0, g1, k0, k1, s0, s1, kept):
    for i, (got, keep, send) in enumerate(((g0, k0, s0), (g1, k1, s1))):
        send[...] = (keep[2:4] + got[2:4].astype(F32)).astype(BF16)
        kept[2 * i : 2 * i + 2] = keep[0:2] + got[0:2].astype(F32)


def line_kernel(g0, g1, keep, send, kept):
    send[...] = (keep[2:4] + g1[...].astype(F32)).astype(BF16)
    kept[...] = keep[0:2] + g0[...].astype(F32)


def last_kernel(got, keep, send, kept):
    send[...] = (keep[1] + got[1].astype(F32)).astype(BF16)
    kept[...] = keep[0] + got[0].astype(F32)


def assemble(me, sx, sy, sz, gx, gy, gz, w):
    mx, my, mz, c = me[0], me[1], me[2], me[3]
    xs = [[reached4(mx, c, a, b) * 512 for b in range(2)] for a in range(2)]
    ys = [[reached4(my, c, a, b) for b in range(2)] for a in range(2)]
    ys = [[(y // 2) * 2048 + lax.rem(y, 2) * 256 for y in row] for row in ys]
    zs = [[reached8(mz, c, a, d) * 32 for d in range(4)] for a in range(2)]
    for xa in range(2):
        for ya in range(2):
            for za in range(2):
                for i in range(16):
                    at = pl.multiple_of(xs[xa][i // 8] + ys[ya][(i // 4) % 2] + zs[za][i % 4], 32)
                    label = (xa, ya, za)

                    def part(stream, sent, got):
                        first, second, third = (label[axis] for axis in AXES[stream])
                        return (got if first else sent)[third * 32 + second * 16 + i]

                    w[pl.ds(at, 16), 0:384] = part(0, sx, gx)
                    w[pl.ds(at + 16, 16), 0:384] = part(1, sy, gy)
                    w[pl.ds(at, 32), 384:512] = part(2, sz, gz)


def other_kernel(me, r0, r1, sx, sy, sz, gx, gy, gz, out, w):
    assemble(me, sx, sy, sz, gx, gy, gz, w)
    for m in range(out.shape[0]):
        total = jnp.dot(r0[m], w[0:2048], preferred_element_type=F32) + jnp.dot(
            r1[m], w[2048:4096], preferred_element_type=F32
        )
        out[m] = total.astype(BF16)


def mine_kernel(me, tokens, w, out):
    columns = [pl.multiple_of(2048 * me[3] + 4096 * i, 2048) for i in range(2)]
    for m in range(out.shape[0]):
        out[m] = jnp.dot(tokens[m, :, pl.ds(columns[0], 2048)], w[0:2048], preferred_element_type=F32) + jnp.dot(
            tokens[m, :, pl.ds(columns[1], 2048)], w[2048:4096], preferred_element_type=F32
        )


def my_values(me, tokens, w):
    return pl.pallas_call(
        mine_kernel,
        in_specs=[SMEM, VMEM, VMEM],
        out_specs=VMEM,
        out_shape=jax.ShapeDtypeStruct((*tokens.shape[:2], 512), F32),
        compiler_params=PARAMS,
        interpret=INTERPRET,
    )(me, tokens, w)


def end_kernel(got, keep, mine, other, grad, values):
    grad[...] = keep[...] + got[...].astype(F32)
    values[...] = (mine[...] + other[...].astype(F32)).astype(BF16)


def other_values(me, r0, r1, messages):
    return pl.pallas_call(
        other_kernel,
        in_specs=[SMEM] + [VMEM] * 8,
        out_specs=[VMEM] * 2,
        out_shape=[
            jax.ShapeDtypeStruct((*r0.shape[:2], 512), BF16),
            jax.ShapeDtypeStruct((4096, 512), BF16),
        ],
        compiler_params=PARAMS,
        interpret=INTERPRET,
    )(me, r0, r1, *messages)


def after(value, *others):
    return lax.optimization_barrier((value, *others))[0]


def body(tokens, cotangent, master, moment, second, gradient):
    node, dp = lax.axis_index("node"), lax.axis_index("dp")
    me = jnp.stack([dp // 16, (node // 2) * 2 + (dp // 8) % 2, dp % 8, node % 2]).astype(jnp.int32)

    in_hbm = (
        pltpu.with_memory_space_constraint(a, pltpu.HBM) for a in (tokens, cotangent, master, moment, second, gradient)
    )
    r0, r1, cotangent, weight, new_master, new_moment, new_second = first(me, *in_hbm)
    cotr, r0, r1 = swap(cotangent), swap(r0), swap(r1)
    far = far_step(weight, 2, True)
    mine = own_terms(me, tokens, cotangent)
    line = jnp.stack(lax.optimization_barrier((weight, far, mine))[:2])
    line = jnp.concatenate([line, far_step(line, 2, False)])
    held = all_terms(me, r0, r1, cotr, mine)
    send, keep = held[:3], held[3:]

    got = [near(send[i], AXES[i][0]) for i in range(3)]
    line = after(line, send[0])
    plane = jnp.concatenate([line, far_step(line, 1, False)])
    plane = jnp.concatenate([plane, far_step(plane, 0, False)])

    *got, plane = lax.optimization_barrier((*got, plane))
    new = [
        call(
            functools.partial(second_kernel, i),
            [message(48, i), ((32, *STREAMS[i]), F32)],
            got[i],
            keep[i],
            plane,
        )
        for i in range(3)
    ]
    send, keep = [n[0] for n in new], [n[1] for n in new]
    got = [near(send[i], AXES[i][1]) for i in range(3)]

    new = [
        call(third_kernel, [message(48, i), ((16, *STREAMS[i]), F32)], got[i], keep[i], send[i])
        for i in range(3)
    ]
    send, keep = [n[0] for n in new], [n[1] for n in new]
    got = [near(send[i], AXES[i][2]) for i in range(3)]

    block = (32, 512)
    s0, s1, k0, k1 = call(far_kernel, [((4, *block), BF16)] * 2 + [((4, *block), F32)] * 2, *got, *keep)
    g0, g1 = far_step(s0, 0, False), far_step(s1, 1, False)
    half = [call(fourth_kernel, [message(64, i)], got[i], send[i])[0] for i in range(3)]
    rest = [near(half[i], AXES[i][0]) for i in range(3)]
    s0, s1, kept = call(across_kernel, [((2, *block), BF16)] * 2 + [((4, *block), F32)], g0, g1, k0, k1)
    g0, g1 = far_step(s0, 1, False), far_step(s1, 0, False)
    s, kept = call(line_kernel, [((2, *block), BF16), ((2, *block), F32)], g0, g1, kept)
    got = far_step(s, 2, False)

    other, w = other_values(after(me, kept), r0, r1, [*half, *rest])
    s, kept = call(last_kernel, [(block, BF16), (block, F32)], got, after(kept, w))
    got = far_step(s, 2, True)
    other = swap(after(other, kept))
    mine = my_values(me, tokens, after(w, kept))
    weight_grad, values = call(
        end_kernel, [(block, F32), ((*r0.shape[:2], 512), BF16)], got, kept, mine, other
    )
    return (new_master, new_moment, new_second, values, weight_grad)


def solution(mesh):
    rows = P(("node", "dp"), None)
    tall = P(None, ("node", "dp"), None)
    return jax.shard_map(
        body,
        mesh=mesh,
        in_specs=(tall, tall, rows, rows, rows, rows),
        out_specs=(rows, rows, rows, tall, rows),
        check_vma=False,
    )
```

```python
import functools
import jax
import jax.numpy as jnp
from jax import lax
from jax.experimental import pallas as pl
from jax.experimental.pallas import tpu as pltpu
from jax.sharding import PartitionSpec as P

F32, BF16 = jnp.float32, jnp.bfloat16
ALL = ("node", "dp")
INTERPRET = False
VMEM = pl.BlockSpec(memory_space=pltpu.VMEM)
SMEM = pl.BlockSpec(memory_space=pltpu.SMEM)
HBM = pl.BlockSpec(memory_space=pltpu.HBM)
PARAMS = pltpu.CompilerParams(vmem_limit_bytes=28 << 20)


STREAMS = ((16, 384), (16, 384), (32, 128))
AXES = ((2, 0, 1), (1, 2, 0), (0, 1, 2))


def message(n, stream):
    return (n + n // 2 if stream == 2 and n == 48 else n, *STREAMS[stream]), BF16


def place(x, y, z, c):
    return ((((y // 2) * 2 + c) * 4 + x) * 2 + y % 2) * 8 + z


def permute(value, move):
    pairs = []
    for c in range(2):
        for x in range(4):
            for y in range(4):
                for z in range(8):
                    pairs.append((place(x, y, z, c), place(*move(x, y, z, c))))
    return lax.ppermute(value, ALL, pairs)


def neighbour(v, n, c):
    return (v + 1 - 2 * ((v + c) % 2)) % n


def near(value, axis):
    def move(x, y, z, c):
        at = [x, y, z]
        at[axis] = neighbour(at[axis], (4, 4, 8)[axis], c)
        return (*at, c)

    return permute(value, move)


def far_step(value, axis, second):
    def move(x, y, z, c):
        at = [x, y, z]
        if axis < 2:
            at[axis] = neighbour(at[axis], 4, 1 - c)
        else:
            w = neighbour((z + c) // 2 % 4, 4, (1 - c) if second else c)
            at[2] = (2 * w + (z % 2) * (1 - 2 * c)) % 8
        return (*at, c)

    return permute(value, move)


def swap(value):
    return permute(value, lambda x, y, z, c: (x, y, z, 1 - c))


def as_int(flag):
    return jnp.where(flag, 1, 0)


def label4(u, v, c):
    step = 1 - 2 * lax.rem(v + c, 2)
    delta = lax.rem(u - v + 4, 4)
    far = delta == 2
    return as_int(far | (delta == lax.rem(step + 4, 4))), as_int(far | (delta == lax.rem(4 - step, 4)))


def label8(u, v, c):
    b, d = label4(lax.rem((u + c) // 2, 4), lax.rem((v + c) // 2, 4), c)
    return lax.rem(u + v, 2), b * 2 + d


def reached4(v, c, a, b):
    step = 1 - 2 * lax.rem(v + c, 2)
    return lax.rem(v + (2 if a and b else a * step - b * step) + 4, 4)


def reached8(v, c, a, d):
    w = reached4(lax.rem((v + c) // 2, 4), c, d // 2, d % 2)
    p = lax.rem(v + a, 2)
    return lax.rem(2 * w + p * (1 - 2 * c) + 8, 8)


def call(kernel, outs, *args, **more):
    return pl.pallas_call(
        kernel,
        out_shape=[jax.ShapeDtypeStruct(*o) for o in outs],
        in_specs=[VMEM] * len(args),
        out_specs=[VMEM] * len(outs),
        compiler_params=PARAMS,
        interpret=INTERPRET,
        **more,
    )(*args)


def load_half(tokens, column, to, sems, at):
    half = tokens.shape[1] // 2
    pieces = [(i, m, h) for i in range(2) for m in range(2) for h in range(2)]
    return [
        pltpu.make_async_copy(
            tokens.at[m, pl.ds(half * h, half), pl.ds(column + 4096 * i, 2048)],
            to[i].at[m, pl.ds(half * h, half)],
            sems.at[at + n],
        )
        for n, (i, m, h) in enumerate(pieces)
    ]


def first_kernel(me, tokens, cot, master, moment, second, gradient, r0, r1, held, weight, out_master, out_moment, out_second, rows, sems):
    far = pl.multiple_of(2048 * (1 - me[3]), 2048)
    loads = [
        pltpu.make_async_copy(ref, rows.at[i], sems.at[i]) for i, ref in enumerate((master, moment, second, gradient))
    ]
    copies = load_half(tokens, far, (r0, r1), sems, 4)
    copies.append(pltpu.make_async_copy(cot, held, sems.at[12]))
    for copy in loads + copies:
        copy.start()
    for copy in loads:
        copy.wait()
    new_moment = 0.9 * rows[1] + 0.1 * rows[3]
    new_second = 0.95 * rows[2] + 0.05 * rows[3] * rows[3]
    first_fix = 1.0 - 0.9**10
    second_fix = 1.0 - 0.95**10
    update = new_moment / first_fix / (jnp.sqrt(new_second / second_fix) + 1e-08) + 0.1 * rows[0]
    new_master = rows[0] - 0.001 * update
    out_master[...] = new_master
    out_moment[...] = new_moment
    out_second[...] = new_second
    weight[...] = new_master.astype(BF16)
    for copy in copies:
        copy.wait()


def first(me, tokens, cot, master, moment, second, gradient):
    half = jax.ShapeDtypeStruct((*tokens.shape[:2], 2048), BF16)
    rows = jax.ShapeDtypeStruct(master.shape, F32)
    return pl.pallas_call(
        first_kernel,
        in_specs=[SMEM] + [HBM] * 6,
        out_specs=[VMEM] * 7,
        out_shape=[half, half, jax.ShapeDtypeStruct(cot.shape, BF16), jax.ShapeDtypeStruct(master.shape, BF16), rows, rows, rows],
        scratch_shapes=[pltpu.VMEM((4, *master.shape), F32), pltpu.SemaphoreType.DMA((13,))],
        compiler_params=PARAMS,
        interpret=INTERPRET,
    )(me, tokens, cot, master, moment, second, gradient)


def product(a, b):
    flat = b.shape[0] * b.shape[1]
    return lax.dot_general(
        a.reshape(flat, 512), b[...].reshape(flat, 512), (((0,), (0,)), ((), ())), preferred_element_type=F32
    )


def own_kernel(me, tokens, cot, out):
    for t in range(8):
        column = pl.multiple_of(2048 * me[3] + 4096 * (t // 4) + 512 * (t % 4), 512)
        out[t] = product(tokens[:, :, pl.ds(column, 512)], cot)


def own_terms(me, tokens, cot):
    return pl.pallas_call(
        own_kernel,
        in_specs=[SMEM, VMEM, VMEM],
        out_specs=VMEM,
        out_shape=jax.ShapeDtypeStruct((8, 512, 512), F32),
        compiler_params=PARAMS,
        interpret=INTERPRET,
    )(me, tokens, cot)


def terms_kernel(me, r0, r1, cot, mine, sx, sy, sz, kx, ky, kz):
    mx, my, mz, c = me[0], me[1], me[2], me[3]
    xs = [label4(x, mx, c) for x in range(4)]
    ys = [label4(y, my, c) for y in range(4)]
    zs = [label8(z, mz, c) for z in range(8)]
    for t in range(8):
        acc = mine[t] + product((r0, r1)[t // 4][:, :, 512 * (t % 4) : 512 * (t % 4) + 512], cot)
        for j in range(16):
            x, y, z = xs[t % 4], ys[2 * (t // 4) + j // 8], zs[j % 8]
            far = x[1] * 8 + y[1] * 4 + z[1]
            axes = (x[0], y[0], z[0])
            block = acc[32 * j : 32 * j + 32]
            for stream, (send, keep) in enumerate(((sx, kx), (sy, ky), (sz, kz))):
                first_, second_, third_ = (axes[axis] for axis in AXES[stream])
                at = second_ * 32 + third_ * 16 + far
                piece = cut(stream, block)
                send[jnp.where(first_ == 1, at, 64)] = piece.astype(BF16)
                keep[jnp.where(first_ == 1, 64, at)] = piece


def all_terms(me, r0, r1, cot, mine):
    return pl.pallas_call(
        terms_kernel,
        in_specs=[SMEM] + [VMEM] * 4,
        out_specs=[VMEM] * 6,
        out_shape=[jax.ShapeDtypeStruct(*message(65, i)) for i in range(3)]
        + [jax.ShapeDtypeStruct((65, *s), F32) for s in STREAMS],
        compiler_params=PARAMS,
        interpret=INTERPRET,
    )(me, r0, r1, cot, mine)


def cut(stream, block):
    return (block[..., 0:16, 0:384], block[..., 16:32, 0:384], block[..., :, 384:512])[stream]


def second_kernel(stream, got, keep, plane, send, kept):
    send[0:32] = (keep[32:64] + got[32:64].astype(F32)).astype(BF16)
    send[32:48] = cut(stream, plane[...])
    kept[...] = keep[0:32] + got[0:32].astype(F32)


def third_kernel(got, keep, sent, send, kept):
    send[0:16] = (keep[16:32] + got[16:32].astype(F32)).astype(BF16)
    send[16:32] = sent[32:48]
    send[32:48] = got[32:48]
    kept[...] = keep[0:16] + got[0:16].astype(F32)


def fourth_kernel(got, sent, send):
    send[0:32] = sent[16:48]
    send[32:64] = got[16:48]


def far_kernel(gx, gy, gz, kx, ky, kz, s0, s1, k0, k1):
    for out, start, stride in ((s0, 8, 4), (k0, 0, 4), (s1, 6, 8), (k1, 2, 8)):
        for i in range(2):
            at, to = slice(start + stride * i, start + stride * i + 2), slice(2 * i, 2 * i + 2)
            out[to, 0:16, 0:384] = (kx[at] + gx[at].astype(F32)).astype(out.dtype)
            out[to, 16:32, 0:384] = (ky[at] + gy[at].astype(F32)).astype(out.dtype)
            out[to, :, 384:512] = (kz[at] + gz[at].astype(F32)).astype(out.dtype)


def across_kernel(g0, g1, k0, k1, s0, s1, kept):
    for i, (got, keep, send) in enumerate(((g0, k0, s0), (g1, k1, s1))):
        send[...] = (keep[2:4] + got[2:4].astype(F32)).astype(BF16)
        kept[2 * i : 2 * i + 2] = keep[0:2] + got[0:2].astype(F32)


def line_kernel(g0, g1, keep, send, kept):
    send[...] = (keep[2:4] + g1[...].astype(F32)).astype(BF16)
    kept[...] = keep[0:2] + g0[...].astype(F32)


def last_kernel(got, keep, send, kept):
    send[...] = (keep[1] + got[1].astype(F32)).astype(BF16)
    kept[...] = keep[0] + got[0].astype(F32)


def assemble(me, sx, sy, sz, gx, gy, gz, w):
    mx, my, mz, c = me[0], me[1], me[2], me[3]
    xs = [[reached4(mx, c, a, b) * 512 for b in range(2)] for a in range(2)]
    ys = [[reached4(my, c, a, b) for b in range(2)] for a in range(2)]
    ys = [[(y // 2) * 2048 + lax.rem(y, 2) * 256 for y in row] for row in ys]
    zs = [[reached8(mz, c, a, d) * 32 for d in range(4)] for a in range(2)]
    for xa in range(2):
        for ya in range(2):
            for za in range(2):
                for i in range(16):
                    at = pl.multiple_of(xs[xa][i // 8] + ys[ya][(i // 4) % 2] + zs[za][i % 4], 32)
                    label = (xa, ya, za)

                    def part(stream, sent, got):
                        first, second, third = (label[axis] for axis in AXES[stream])
                        return (got if first else sent)[third * 32 + second * 16 + i]

                    w[pl.ds(at, 16), 0:384] = part(0, sx, gx)
                    w[pl.ds(at + 16, 16), 0:384] = part(1, sy, gy)
                    w[pl.ds(at, 32), 384:512] = part(2, sz, gz)


def other_kernel(me, r0, r1, sx, sy, sz, gx, gy, gz, out, w):
    assemble(me, sx, sy, sz, gx, gy, gz, w)
    for m in range(out.shape[0]):
        total = jnp.dot(r0[m], w[0:2048], preferred_element_type=F32) + jnp.dot(
            r1[m], w[2048:4096], preferred_element_type=F32
        )
        out[m] = total.astype(BF16)


def mine_kernel(me, tokens, w, out):
    columns = [pl.multiple_of(2048 * me[3] + 4096 * i, 2048) for i in range(2)]
    for m in range(out.shape[0]):
        out[m] = jnp.dot(tokens[m, :, pl.ds(columns[0], 2048)], w[0:2048], preferred_element_type=F32) + jnp.dot(
            tokens[m, :, pl.ds(columns[1], 2048)], w[2048:4096], preferred_element_type=F32
        )


def my_values(me, tokens, w):
    return pl.pallas_call(
        mine_kernel,
        in_specs=[SMEM, VMEM, VMEM],
        out_specs=VMEM,
        out_shape=jax.ShapeDtypeStruct((*tokens.shape[:2], 512), F32),
        compiler_params=PARAMS,
        interpret=INTERPRET,
    )(me, tokens, w)


def end_kernel(got, keep, mine, other, grad, values):
    grad[...] = keep[...] + got[...].astype(F32)
    values[...] = (mine[...] + other[...].astype(F32)).astype(BF16)


def other_values(me, r0, r1, messages):
    return pl.pallas_call(
        other_kernel,
        in_specs=[SMEM] + [VMEM] * 8,
        out_specs=[VMEM] * 2,
        out_shape=[
            jax.ShapeDtypeStruct((*r0.shape[:2], 512), BF16),
            jax.ShapeDtypeStruct((4096, 512), BF16),
        ],
        compiler_params=PARAMS,
        interpret=INTERPRET,
    )(me, r0, r1, *messages)


def after(value, *others):
    return lax.optimization_barrier((value, *others))[0]


def body(tokens, cotangent, master, moment, second, gradient):
    node, dp = lax.axis_index("node"), lax.axis_index("dp")
    me = jnp.stack([dp // 16, (node // 2) * 2 + (dp // 8) % 2, dp % 8, node % 2]).astype(jnp.int32)

    in_hbm = (
        pltpu.with_memory_space_constraint(a, pltpu.HBM) for a in (tokens, cotangent, master, moment, second, gradient)
    )
    r0, r1, cotangent, weight, new_master, new_moment, new_second = first(me, *in_hbm)
    cotr, r0, r1 = swap(cotangent), swap(r0), swap(r1)
    far = far_step(weight, 2, True)
    mine = own_terms(me, tokens, cotangent)
    line = jnp.stack(lax.optimization_barrier((weight, far, mine))[:2])
    line = jnp.concatenate([line, far_step(line, 2, False)])
    held = all_terms(me, r0, r1, cotr, mine)
    send, keep = held[:3], held[3:]

    got = [near(send[i], AXES[i][0]) for i in range(3)]
    line = after(line, send[0])
    plane = jnp.concatenate([line, far_step(line, 1, False)])
    plane = jnp.concatenate([plane, far_step(plane, 0, False)])

    *got, plane = lax.optimization_barrier((*got, plane))
    new = [
        call(
            functools.partial(second_kernel, i),
            [message(48, i), ((32, *STREAMS[i]), F32)],
            got[i],
            keep[i],
            plane,
        )
        for i in range(3)
    ]
    send, keep = [n[0] for n in new], [n[1] for n in new]
    got = [near(send[i], AXES[i][1]) for i in range(3)]

    new = [
        call(third_kernel, [message(48, i), ((16, *STREAMS[i]), F32)], got[i], keep[i], send[i])
        for i in range(3)
    ]
    send, keep = [n[0] for n in new], [n[1] for n in new]
    got = [near(send[i], AXES[i][2]) for i in range(3)]

    block = (32, 512)
    s0, s1, k0, k1 = call(far_kernel, [((4, *block), BF16)] * 2 + [((4, *block), F32)] * 2, *got, *keep)
    g0, g1 = far_step(s0, 0, False), far_step(s1, 1, False)
    half = [call(fourth_kernel, [message(64, i)], got[i], send[i])[0] for i in range(3)]
    rest = [near(half[i], AXES[i][0]) for i in range(3)]
    s0, s1, kept = call(across_kernel, [((2, *block), BF16)] * 2 + [((4, *block), F32)], g0, g1, k0, k1)
    g0, g1 = far_step(s0, 1, False), far_step(s1, 0, False)
    s, kept = call(line_kernel, [((2, *block), BF16), ((2, *block), F32)], g0, g1, kept)
    got = far_step(s, 2, False)

    other, w = other_values(after(me, kept), r0, r1, [*half, *rest])
    s, kept = call(last_kernel, [(block, BF16), (block, F32)], got, after(kept, w))
    got = far_step(s, 2, True)
    other = swap(after(other, kept))
    mine = my_values(me, tokens, after(w, kept))
    weight_grad, values = call(
        end_kernel, [(block, F32), ((*r0.shape[:2], 512), BF16)], got, kept, mine, other
    )
    return (new_master, new_moment, new_second, values, weight_grad)


def solution(mesh):
    rows = P(("node", "dp"), None)
    tall = P(None, ("node", "dp"), None)
    return jax.shard_map(
        body,
        mesh=mesh,
        in_specs=(tall, tall, rows, rows, rows, rows),
        out_specs=(rows, rows, rows, tall, rows),
        check_vma=False,
    )
```
